128 devices in a mesh: dp: 32 (over y, x_hi, z), tensor: 4 (over x_lo, core).
Axes of the slice: x: 4 (x_hi: 2, x_lo: 2; x = x_hi * 2 + x_lo), y: 4, z: 4, core: 2. Of those that a mesh axis runs over, the one named last changes fastest.
Arguments:
- prompt_x: bfloat16 [4096, 5120], P('dp', 'tensor'), may hold values from -6 to 6
- prompt_bc: bfloat16 [4096, 512], P('dp'), may hold values from -6 to 6
- prompt_dt: float32 [80, 4096], P('tensor', 'dp'), may hold values from -2.5 to 6.5
- prompt_z: bfloat16 [4096, 5120], P('dp', 'tensor'), may hold values from -6 to 6
- resp_x: bfloat16 [16384, 5120], P('dp', 'tensor'), may hold values from -6 to 6
- resp_bc: bfloat16 [16384, 512], P('dp'), may hold values from -6 to 6
- resp_dt: float32 [80, 16384], P('tensor', 'dp'), may hold values from -2.5 to 6.5
- resp_z: bfloat16 [16384, 5120], P('dp', 'tensor'), may hold values from -6 to 6
- conv_x: float32 [4, 5120], P(None, 'tensor'), may hold values from -3 to 3
- conv_bc: float32 [4, 512], replicated, may hold values from -3 to 3
- head_params: float32 [3, 80], P(None, 'tensor'), may hold values from -8 to 1.5, as said below
- prompt_of: int32 [32], replicated, may hold values from 0 to 31, each once
- resp_len: int32 [32, 4], P('dp'), may hold values from 32 to 128, as said below
- prompt_cot: bfloat16 [4096, 5120], P('dp', 'tensor'), may hold values from -6 to 6
- resp_cot: bfloat16 [16384, 5120], P('dp', 'tensor'), may hold values from -6 to 6
Outputs:
- resp_out: bfloat16 [16384, 5120], P('dp', 'tensor')
- prompt_grad_x: bfloat16 [4096, 5120], P('dp', 'tensor')
- prompt_grad_bc: float32 [4096, 512], P('dp')
- prompt_grad_dt: float32 [80, 4096], P('tensor', 'dp')
- resp_grad_x: bfloat16 [16384, 5120], P('dp', 'tensor')
- resp_grad_bc: float32 [16384, 512], P('dp')
- resp_grad_dt: float32 [80, 16384], P('tensor', 'dp')
- conv_x_grad: float32 [4, 5120], P(None, 'tensor')
- conv_bc_grad: float32 [4, 512], replicated
- head_grads: float32 [3, 80], P(None, 'tensor')
The draws below stay inside these ranges and needn't reach their ends.
Inputs may be any that keep to these rules, and one draw needn't show every extreme that they name: prompt_of is a permutation: every prompt is continued on exactly one dp index. `resp_len`: every dp index has at least one response of the full 128 tokens. `head_params`: row 0 is a log rate, row 1 a step bias below zero, row 2 a skip gain.
All inputs are finite; a program needn't handle non-finite values.
Results may differ from the reference program's by a relative error of at most 0.0045.
Values sent between devices are 32-bit elements; how exact they have to be, the bound alone decides.
A program may use at most 192 MiB of HBM per device.

```python
import jax
import jax.numpy as jnp
from jax import lax

HEADS = 80
HEAD = 64
STATE = 256
CONV = 4
SPAN = 128
P_DEV = 128
RESPONSES = 4
RESP_LEN = 128
CH = 5120
BC = 512
P_TOKENS = 4096
R_TOKENS = 16384
N_DP = 32


def spike_rows(key, column_list):
    struck = jax.random.uniform(key, (1, column_list)) < 1.0 / 128.0
    return jnp.where(struck, 4.0, 0.0)


def draw_prompt_dt(key, part):
    key = jax.random.fold_in(key, 11)
    key_noise, key_spike = jax.random.split(key)
    column_list = N_DP * P_DEV
    random_noise = jnp.clip(0.5 * jax.random.normal(key_noise, (HEADS, column_list)), -2.5, 2.5)
    return (random_noise + spike_rows(key_spike, column_list)).astype(jnp.float32)


def draw_resp_dt(key, part):
    key = jax.random.fold_in(key, 12)
    key_noise, key_spike = jax.random.split(key)
    column_list = N_DP * RESPONSES * RESP_LEN
    random_noise = jnp.clip(0.5 * jax.random.normal(key_noise, (HEADS, column_list)), -2.5, 2.5)
    return (random_noise + spike_rows(key_spike, column_list)).astype(jnp.float32)


def log_uniform(key, lower_end, upper_end):
    return jnp.exp(jax.random.uniform(key, (HEADS,), minval=jnp.log(lower_end), maxval=jnp.log(upper_end)))


def draw_head_params(key, part):
    key = jax.random.fold_in(key, 13)
    key_rate, key_step, key_skip = jax.random.split(key, 3)
    rates = log_uniform(key_rate, 0.5, 2.0)
    base_step = log_uniform(key_step, 0.002, 0.03)
    skips = jax.random.uniform(key_skip, (HEADS,), minval=0.5, maxval=1.5)
    return jnp.stack([jnp.log(rates), jnp.log(jnp.expm1(base_step)), skips]).astype(jnp.float32)


def draw_resp_len(key, part):
    key = jax.random.fold_in(key, 17)
    key_len, key_pick = jax.random.split(key)
    lengths = jax.random.randint(key_len, (N_DP, RESPONSES), RESP_LEN // 4, RESP_LEN + 1)
    picked = jax.random.randint(key_pick, (N_DP, 1), 0, RESPONSES)
    longest = jnp.arange(RESPONSES)[None, :] == picked
    return jnp.where(longest, RESP_LEN, lengths).astype(jnp.int32)


def shard_levels(own_key, shape, shards, least, high):
    loudness = 1.0
    for axis_at, blocks in shards:
        draws = jax.random.uniform(jax.random.fold_in(jax.random.fold_in(own_key, 6), axis_at), (blocks,), jnp.float32, least / len(shards), high / len(shards))
        loudness = loudness * jnp.repeat(jnp.exp(draws), shape[axis_at] // blocks).reshape((-1,) + (1,) * (len(shape) - 1 - axis_at))
    return loudness


def noise(rng, extent, deviation, limit, pieces=(), dtype=jnp.bfloat16):
    values = deviation * jax.random.normal(rng, extent, jnp.float32)
    if pieces:
        values = values * shard_levels(rng, extent, pieces, -0.22, 0.18)
    return jnp.clip(values, -limit, limit).astype(dtype)


def setup_inputs(seed: int = 0) -> dict:
    streams_of = jax.random.split(jax.random.key(seed), 16)
    return {
        "prompt_x": noise(streams_of[0], (P_TOKENS, CH), 1.0, 6.0, ((0, 32), (1, 4))),
        "prompt_bc": noise(streams_of[1], (P_TOKENS, BC), 1.0, 6.0, ((0, 32),)),
        "prompt_dt": draw_prompt_dt(jax.random.fold_in(streams_of[15], 71), 0),
        "prompt_z": noise(streams_of[3], (P_TOKENS, CH), 1.0, 6.0, ((0, 32), (1, 4))),
        "resp_x": noise(streams_of[4], (R_TOKENS, CH), 1.0, 6.0, ((0, 32), (1, 4))),
        "resp_bc": noise(streams_of[5], (R_TOKENS, BC), 1.0, 6.0, ((0, 32),)),
        "resp_dt": draw_resp_dt(jax.random.fold_in(streams_of[15], 71), 0),
        "resp_z": noise(streams_of[7], (R_TOKENS, CH), 1.0, 6.0, ((0, 32), (1, 4))),
        "conv_x": noise(streams_of[8], (CONV, CH), CONV ** -0.5, 3.0, ((1, 4),), jnp.float32),
        "conv_bc": noise(streams_of[9], (CONV, BC), CONV ** -0.5, 3.0, (), jnp.float32),
        "head_params": draw_head_params(jax.random.fold_in(streams_of[15], 71), 0),
        "prompt_of": jax.random.permutation(streams_of[11], N_DP).astype(jnp.int32),
        "resp_len": draw_resp_len(jax.random.fold_in(streams_of[15], 71), 0),
        "prompt_cot": noise(streams_of[13], (P_TOKENS, CH), 1.0, 6.0, ((0, 32), (1, 4))),
        "resp_cot": noise(streams_of[14], (R_TOKENS, CH), 1.0, 6.0, ((0, 32), (1, 4))),
    }


def conv_silu(raw_rows, trailing_rows, kernel):
    extended = jnp.concatenate([trailing_rows, raw_rows], axis=0)
    length = raw_rows.shape[0]
    summed = jnp.zeros(raw_rows.shape, jnp.float32)
    for offset in range(kernel.shape[0]):
        summed = summed + kernel[offset][None, :] * extended[offset:offset + length]
    return jax.nn.silu(summed)

def state_mixer(feat_conv, proj_conv, step_raw, gate_rows, params, start_state):
    head_count = params.shape[1]
    state_dim = proj_conv.shape[1] // 2
    length = feat_conv.shape[0]
    blocks = length // SPAN
    step_size = jax.nn.softplus(step_raw + params[1][:, None])
    log_decay = -jnp.exp(params[0])[:, None] * step_size
    feat_blocks = feat_conv.reshape(blocks, SPAN, head_count, HEAD)
    write_blocks = proj_conv[:, :state_dim].reshape(blocks, SPAN, state_dim)
    read_blocks = proj_conv[:, state_dim:].reshape(blocks, SPAN, state_dim)
    step_blocks = step_size.reshape(head_count, blocks, SPAN).transpose(1, 0, 2)
    rate_blocks = log_decay.reshape(head_count, blocks, SPAN).transpose(1, 0, 2)
    lower = jnp.arange(SPAN)[:, None] >= jnp.arange(SPAN)[None, :]
    skip_gain = params[2][None, :, None]

    def advance(carry_state, block):
        feat_rows, write_rows, read_rows, step_rows, rate_rows = block
        cumulative = jnp.cumsum(rate_rows, axis=1)
        differ = cumulative[:, :, None] - cumulative[:, None, :]
        within = jnp.where(lower[None], jnp.exp(jnp.minimum(differ, 0.0)), 0.0)
        scores = jnp.dot(read_rows, write_rows.T, precision=lax.Precision.HIGHEST)
        mixing = scores[None] * within * step_rows[:, None, :]
        inside = jnp.einsum('hts,shp->thp', mixing, feat_rows, precision=lax.Precision.HIGHEST)
        carried = jnp.einsum('tn,hpn->thp', read_rows, carry_state, precision=lax.Precision.HIGHEST)
        carried = carried * jnp.exp(cumulative).T[:, :, None]
        outputs = inside + carried + skip_gain * feat_rows
        leaving = (jnp.exp(cumulative[:, -1:] - cumulative) * step_rows).T
        update = jnp.einsum('sn,shp->hpn', write_rows, feat_rows * leaving[:, :, None], precision=lax.Precision.HIGHEST)
        carry_state = jnp.exp(cumulative[:, -1])[:, None, None] * carry_state + update
        return (carry_state, outputs)
    final_state, outputs = lax.scan(jax.checkpoint(advance), start_state, (feat_blocks, write_blocks, read_blocks, step_blocks, rate_blocks))
    mixed = outputs.reshape(length, head_count * HEAD) * jax.nn.silu(gate_rows)
    return (mixed, final_state)

def reference(prompt_x, prompt_bc, prompt_dt, prompt_z, resp_x, resp_bc, resp_dt, resp_z, conv_x, conv_bc, head_params, prompt_of, resp_len, prompt_cot, resp_cot):
    channels = prompt_x.shape[1]
    bc_width = prompt_bc.shape[1]
    tail_len = CONV - 1
    prompt_gate = prompt_z.astype(jnp.float32).reshape(N_DP, P_DEV, channels)
    resp_gate = resp_z.astype(jnp.float32).reshape(N_DP, RESPONSES, RESP_LEN, channels)
    zero_feat = jnp.zeros((tail_len, channels), jnp.float32)
    zero_proj = jnp.zeros((tail_len, bc_width), jnp.float32)
    zero_state = jnp.zeros((HEADS, HEAD, STATE), jnp.float32)

    def forward(prompt_feat, prompt_proj, prompt_steps, resp_feat, resp_proj, resp_steps, kernel_feat, kernel_proj, params):
        prompt_parts = (prompt_feat.reshape(N_DP, P_DEV, channels), prompt_proj.reshape(N_DP, P_DEV, bc_width), prompt_steps.reshape(HEADS, N_DP, P_DEV).transpose(1, 0, 2), prompt_gate)

        def one_prompt(parts):
            feat_rows, proj_rows, step_rows, gate_rows = parts
            mixed, final_state = state_mixer(conv_silu(feat_rows, zero_feat, kernel_feat), conv_silu(proj_rows, zero_proj, kernel_proj), step_rows, gate_rows, params, zero_state)
            return (mixed, final_state, feat_rows[-tail_len:], proj_rows[-tail_len:])
        prompt_out, final_states, tails_feat, tails_proj = lax.map(one_prompt, prompt_parts)
        device_parts = (resp_feat.reshape(N_DP, RESPONSES, RESP_LEN, channels), resp_proj.reshape(N_DP, RESPONSES, RESP_LEN, bc_width), resp_steps.reshape(HEADS, N_DP, RESPONSES, RESP_LEN).transpose(1, 2, 0, 3), resp_gate, final_states[prompt_of], tails_feat[prompt_of], tails_proj[prompt_of])

        def one_device(parts):
            feat_set, proj_set, step_set, gate_set, start_state, tail_feat, tail_proj = parts

            def one_response(single):
                feat_rows, proj_rows, step_rows, gate_rows = single
                return state_mixer(conv_silu(feat_rows, tail_feat, kernel_feat), conv_silu(proj_rows, tail_proj, kernel_proj), step_rows, gate_rows, params, start_state)[0]
            return lax.map(one_response, (feat_set, proj_set, step_set, gate_set))
        resp_out = lax.map(one_device, device_parts)
        return (prompt_out.reshape(-1, channels), resp_out.reshape(-1, channels))
    results, pullback = jax.vjp(forward, prompt_x.astype(jnp.float32), prompt_bc.astype(jnp.float32), prompt_dt, resp_x.astype(jnp.float32), resp_bc.astype(jnp.float32), resp_dt, conv_x, conv_bc, head_params)
    live_mask = (jnp.arange(RESP_LEN)[None, None, :] < resp_len[:, :, None]).astype(jnp.float32).reshape(-1, 1)
    gradients = pullback((prompt_cot.astype(jnp.float32), resp_cot.astype(jnp.float32) * live_mask))
    return (results[1].astype(jnp.bfloat16), gradients[0].astype(jnp.bfloat16), gradients[1], gradients[2], gradients[3].astype(jnp.bfloat16), gradients[4], gradients[5], gradients[6], gradients[7], gradients[8])
```

```python
import functools
import types

import jax
import jax.numpy as jnp
from jax import lax
from jax.experimental import pallas as pl
from jax.experimental.pallas import tpu as pltpu
from jax.sharding import PartitionSpec as P

F32 = jnp.float32
BF = jnp.bfloat16
T = 128
NH = 20
NG = 10
NS = 256
CHD = 1280
BCW = 512
CHUNK = 48


def mm(a, b, ca, cb):
    return lax.dot_general(a, b, (((ca,), (cb,)), ((), ())), preferred_element_type=F32)


def split2(a):
    hi = a.astype(BF)
    return hi, (a - hi.astype(F32)).astype(BF)


def split3(a):
    hi = a.astype(BF)
    rest = a - hi.astype(F32)
    mid = rest.astype(BF)
    return hi, mid, (rest - mid.astype(F32)).astype(BF)


def mm3(a, b, ca, cb):
    ah, al = split2(a)
    bh, bl = split2(b)
    return mm(ah, bh, ca, cb) + mm(ah, bl, ca, cb) + mm(al, bh, ca, cb)


def mmx(a, ones, ca, cb):
    hi, mid, lo = split3(a)
    return mm(hi, ones, ca, cb) + mm(mid, ones, ca, cb) + mm(lo, ones, ca, cb)


def sigmoid(v):
    return 0.5 + 0.5 * jnp.tanh(0.5 * v)


def softplus(u):
    e = jnp.exp(-jnp.abs(u))
    s = e / (2.0 + e)
    q = s * s
    poly = 1.0 + q * (1 / 3 + q * (1 / 5 + q * (1 / 7 + q * (1 / 9 + q * (1 / 11 + q / 13)))))
    return jnp.maximum(u, 0.0) + 2.0 * s * poly


def iota(shape, dim):
    return lax.broadcasted_iota(jnp.int32, shape, dim)


def fold8(a):
    return jnp.sum(a.reshape(16, 8, 128), axis=0)


IN = (
    "px", "pbc", "pdt", "pz", "pcot", "rx", "rbc", "rdt", "rz", "rcot", "cw", "cbc", "hp", "of", "inv", "rlen",
)
OUT = (
    "o_out", "o_pdx", "o_pdbc", "o_pddt", "o_rdx", "o_rdbc", "o_rddt", "o_cw", "o_cbc", "o_hp",
)


def scratch_table(n):
    v = pltpu.VMEM
    dma = pltpu.SemaphoreType.DMA
    return dict(
        fs=v((n, CHUNK, 128), F32), fh=v((n, CHUNK, 128), F32), fl=v((n, CHUNK, 128), F32), fr=v((n, CHUNK, 128), F32),
        bs=v((n, CHUNK, 128), F32), bh=v((n, CHUNK, 128), F32), bl=v((n, CHUNK, 128), F32), br=v((n, CHUNK, 128), F32),
        ts=v((32, 2, 128), F32), th=v((32, 2, 128), F32), tl=v((32, 2, 128), F32), tr=v((32, 2, 128), F32),
        us=v((32, 2, 128), F32), uh=v((32, 2, 128), F32), ul=v((32, 2, 128), F32), ur=v((32, 2, 128), F32),
        ps=v((32, 2, 128), F32), ph=v((32, 2, 128), F32), pr=v((32, 2, 128), F32),
        rsum=v((512, BCW), F32), rrecv=v((2, 256, BCW), F32),
        psum=v((144, BCW), F32), pfull=v((144, BCW), F32), precv=v((2, 72, BCW), F32),
        dtr=v((5, NH, T), F32), sig=v((5, NH, T), F32), lr=v((5, NH, T), F32), cumr=v((5, NH, T), F32),
        tmp=v((128, 128), F32), col=v((2, NH, 1), F32), dex=v((1, CHD), F32),
        cumB=v((5 * NH, T, T), F32), dtE=v((5 * T, CHD), F32),
        R=v((NG, 512, 128), BF),
        B=v((5, T, NS), F32), C=v((5, T, NS), F32), Cb=v((5, T, NS), BF), gpb=v((5 * T, BCW), F32),
        G=v((5, T, T), F32), dG=v((5, T, T), F32), acc=v((5, T, 128), F32), accq=v((T, 128), F32),
        xs=v((136, 128), F32), ds=v((144, 128), F32),
        tailx=v((8, CHD), F32), tailb=v((8, BCW), F32), dtailx=v((8, CHD), F32), dtailb=v((8, BCW), F32),
        dw=v((4, 8, CHD), F32), dwb=v((4, 8, BCW), F32), dD=v((8, CHD), F32),
        pxc=v((T, CHD), F32), pgp=v((T, CHD), F32), pdy=v((T, CHD), F32), pdxd=v((T, CHD), F32),
        yl=v((512, CHD), F32), edy=v((512, CHD), BF), ee=v((512, CHD), F32),
        S=v((CHD, NS), BF), dS=v((CHD, NS), BF),
        dlr=v((NH, T), F32), ddr=v((NH, T), F32),
        sem=dma((8, 2, 32)), tsem=dma((6, 2)),
    )


def kernel(n, nt, *refs):
    names = list(IN) + list(OUT) + list(scratch_table(n))
    K = types.SimpleNamespace(**dict(zip(names, refs)))
    me = lax.axis_index("dp")
    mt = lax.axis_index("tensor")
    left = iota((T, 128), 1) < 64

    def spread(src, dst, sem, width=None):
        def copy(k):
            peer = lax.rem(me + k, n)
            return pltpu.make_async_remote_copy(
                src_ref=src(peer), dst_ref=dst, send_sem=K.sem.at[sem, 0, k], recv_sem=K.sem.at[sem, 1, k],
                device_id={"dp": peer}, device_id_type=pl.DeviceIdType.MESH,
            )

        return copy

    def each_peer(action):
        if n > 1:
            pl.loop(1, n)(action)

    def start_all(copy):
        each_peer(lambda k: copy(k).start())

    def wait_all(copy):
        each_peer(lambda k: copy(k).wait())

    def choose(table, hold, sel):
        if n == 1:
            source = {id(K.th): K.ts, id(K.fh): K.fs, id(K.bh): K.bs, id(K.uh): K.us}[id(hold)]
            target = {id(K.th): K.tr, id(K.fh): K.fr, id(K.bh): K.br, id(K.uh): K.ur}[id(hold)]
            target[...] = source[...]
            sel[...] = source[...]
            return

        def one(d):
            sel[d] = hold[table[d]]

        pl.loop(0, n)(one)

    if n > 1:
        barrier = pltpu.get_barrier_semaphore()

        def greet(k):
            pl.semaphore_signal(
                barrier, inc=1, device_id={"dp": lax.rem(me + k, n)}, device_id_type=pl.DeviceIdType.MESH
            )

        each_peer(greet)
        for k in range(1, nt):
            pl.semaphore_signal(
                barrier, inc=1, device_id={"tensor": lax.rem(mt + k, nt)}, device_id_type=pl.DeviceIdType.MESH
            )

    tail_tile_x = K.px[112:128, :].astype(F32)
    tail_tile_b = K.pbc[112:128, :].astype(F32)
    K.ts[...] = jnp.zeros((32, 2, 128), F32)
    for r in range(42):
        i, m = divmod(r, 14)
        part = tail_tile_x[13 + i : 14 + i, 128 * m : 128 * m + 128] if m < 10 else (
            tail_tile_b[13 + i : 14 + i, 128 * (m - 10) : 128 * (m - 10) + 128]
        )
        K.ts[r // 2, r % 2 : r % 2 + 1, :] = part

    t1 = spread(lambda p: K.ts.at[p], K.th.at[me], 0)
    if n > 1:
        pl.semaphore_wait(barrier, n - 1 + nt - 1)
    start_all(t1)

    tri = (iota((T, T), 0) <= iota((T, T), 1)).astype(F32).astype(BF)
    trir = (iota((T, T), 0) >= iota((T, T), 1)).astype(F32).astype(BF)
    tris = (iota((T, T), 0) < iota((T, T), 1)).astype(F32).astype(BF)
    lower = iota((T, T), 0) >= iota((T, T), 1)
    eye = iota((NH, NH), 0) == iota((NH, NH), 1)

    def column(row):
        return jnp.sum(jnp.where(eye, jnp.broadcast_to(K.hp[row : row + 1, :], (NH, NH)), 0.0), axis=1, keepdims=True)

    K.col[0] = -jnp.exp(column(0))
    K.col[1] = column(1)
    left1 = iota((1, 128), 1) < 64
    for g in range(NG):
        K.dex[:, 128 * g : 128 * g + 128] = jnp.where(
            left1, K.hp[2:3, 2 * g : 2 * g + 1], K.hp[2:3, 2 * g + 1 : 2 * g + 2]
        )

    def make_R(g):
        r = iota((512, 128), 0)
        lane = iota((512, 128), 1)
        want = 2 * g + jnp.where((r & 127) >= 64, 1, 0) + jnp.where(r >= 256, 32, 0)
        K.R[g] = (lane == want).astype(F32).astype(BF)

    pl.loop(0, NG)(make_R)
    for name in ("dG", "acc", "accq", "dw", "dwb", "dD", "dtailx", "dtailb", "dlr", "ddr", "ds", "tmp"):
        ref = getattr(K, name)
        ref[...] = jnp.zeros(ref.shape, F32)

    def step_tables(dt_ref, at, q):
        u = dt_ref[:, pl.ds(pl.multiple_of(at * T, T), T)] + K.col[1]
        dt = softplus(u)
        lr = K.col[0] * dt
        cum = mmx(lr, tri, 1, 0)
        K.dtr[q] = dt
        K.sig[q] = 1.0 / (1.0 + jnp.exp(-u))
        K.lr[q] = lr
        K.cumr[q] = cum
        K.tmp[0:NH, :] = cum
        K.tmp[32 : 32 + NH, :] = dt
        cols = K.tmp[...].T
        for h in range(NH):
            K.cumB[q * NH + h] = jnp.broadcast_to(cols[:, h : h + 1], (T, T))
        for g in range(NG):
            a = 32 + 2 * g
            K.dtE[pl.ds(pl.multiple_of(q * T, T), T), 128 * g : 128 * g + 128] = jnp.where(
                left, jnp.broadcast_to(cols[:, a : a + 1], (T, 128)), jnp.broadcast_to(cols[:, a + 1 : a + 2], (T, 128))
            )

    def conv(x, tail, w):
        K.xs[0:8, :] = tail
        K.xs[8:136, :] = x
        v = w[0] * K.xs[5:133, :] + w[1] * K.xs[6:134, :] + w[2] * K.xs[7:135, :] + w[3] * x
        s = sigmoid(v)
        xc = v * s
        return xc, s + xc * (1.0 - s)

    def conv_back(dv, w, dw_ref, lanes, tail_ref):
        K.ds[8:136, :] = dv
        dx = w[3] * dv + w[2] * K.ds[9:137, :] + w[1] * K.ds[10:138, :] + w[0] * K.ds[11:139, :]
        for k in range(4):
            x = K.xs[5 + k : 133 + k, :]
            dw_ref[k, :, lanes] += fold8(dv * x)
        if tail_ref is not None:
            tail_ref[:, lanes] += w[0] * K.ds[3:11, :] + w[1] * K.ds[2:10, :] + w[2] * K.ds[1:9, :]
        return dx

    def taps(ref, lanes):
        return [ref[k : k + 1, lanes] for k in range(4)]

    def lanes_of(g):
        return pl.ds(pl.multiple_of(g * 128, 128), 128)

    def rows_of(q):
        return pl.ds(pl.multiple_of(q * T, T), T)

    def bc_forward(bc_ref, at, q, tail):
        for m in range(4):
            lanes = slice(128 * m, 128 * m + 128)
            xc, gp = conv(bc_ref[rows_of(at), lanes].astype(F32), tail(lanes), taps(K.cbc, lanes))
            K.gpb[rows_of(q), lanes] = gp
            if m < 2:
                K.B[q, :, lanes] = xc
            else:
                half = slice(128 * (m - 2), 128 * (m - 2) + 128)
                K.C[q, :, half] = xc
                K.Cb[q, :, half] = xc.astype(BF)
        K.G[q] = jnp.where(lower, mm3(K.C[q], K.B[q], 1, 1), 0.0)

    def cum_pair(q, g):
        return jnp.where(left, K.cumB[q * NH + 2 * g], K.cumB[q * NH + 2 * g + 1])

    def attend(q, g, xc, dy, dt):
        xd = dt * xc
        x2 = jnp.concatenate([jnp.where(left, xd, 0.0).astype(BF), jnp.where(left, 0.0, xd).astype(BF)], axis=0)
        d2 = jnp.concatenate([jnp.where(left, dy, 0.0).astype(BF), jnp.where(left, 0.0, dy).astype(BF)], axis=0)
        xdb = xd.astype(BF)
        dyb = dy.astype(BF)
        scores = K.G[q]
        decay = [
            jnp.exp(jnp.minimum(K.cumB[q * NH + 2 * g + i] - K.cumr[q, pl.ds(2 * g + i, 1), :], 0.0)) for i in range(2)
        ]
        mix = [(scores * one).astype(BF) for one in decay]
        yin = mm(jnp.concatenate(mix, axis=1), x2, 1, 0)
        dxd = mm(jnp.concatenate(mix, axis=0), d2, 0, 0)
        dmix = mm(dyb, x2, 1, 1)
        K.dG[q] += dmix[:, :T] * decay[0] + dmix[:, T:] * decay[1]
        return yin, dxd, xdb.astype(F32), dyb.astype(F32)

    def reduce_heads(g, first, second=None):
        parts = list(split2(first))
        if second is not None:
            parts += split2(second)
        return mm(jnp.concatenate(parts, axis=1), K.R[g, : 128 * len(parts), :], 1, 0)

    step_tables(K.pdt, 0, 0)
    bc_forward(K.pbc, 0, 0, lambda lanes: jnp.zeros((8, 128), F32))

    def prompt_pre(g):
        lanes = lanes_of(g)
        xc, gp = conv(K.px[:, lanes].astype(F32), jnp.zeros((8, 128), F32), taps(K.cw, lanes))
        K.pxc[:, lanes] = xc
        K.pgp[:, lanes] = gp
        cum = cum_pair(0, g)
        xw = jnp.exp(cum[T - 1 : T, :] - cum) * (K.dtE[0:T, lanes] * xc)
        spot = pl.ds(pl.multiple_of(8 * lax.rem(g, 5), 8), 8)
        for i in range(16):
            K.fs[2 * i + g // 5, spot, :] = xw[8 * i : 8 * i + 8, :]

    pl.loop(0, NG)(prompt_pre)
    for c in range(32):
        K.fs[c, 40:48, :] = K.B[0, 8 * (c // 2) : 8 * (c // 2) + 8, 128 * (c % 2) : 128 * (c % 2) + 128]

    wait_all(t1)
    K.th[me] = K.ts[me]
    choose(K.of, K.th, K.tl)
    t2 = spread(lambda p: K.tl.at[p], K.tr.at[me], 1)
    start_all(t2)
    f1 = spread(lambda p: K.fs.at[p], K.fh.at[me], 2)
    start_all(f1)
    K.tr[me] = K.tl[me]
    K.fh[me] = K.fs[me]

    def prompt_local(g):
        lanes = lanes_of(g)
        xc = K.pxc[:, lanes]
        z = K.pz[:, lanes].astype(F32)
        dy = K.pcot[:, lanes].astype(F32) * (z * sigmoid(z))
        yin, dxd, xdr, dyr = attend(0, g, xc, dy, K.dtE[0:T, lanes])
        K.acc[0] += reduce_heads(g, dyr * yin - xdr * dxd, xc * dxd)
        K.pdxd[:, lanes] = dxd
        K.pdy[:, lanes] = dy
        K.dD[:, lanes] += fold8(dy * xc)

    def resp_tables(j):
        step_tables(K.rdt, j, j + 1)

    pl.loop(0, 4)(resp_tables)
    wait_all(t2)
    K.tailx[...] = jnp.zeros((8, CHD), F32)
    K.tailb[...] = jnp.zeros((8, BCW), F32)
    for r in range(42):
        i, m = divmod(r, 14)
        row = K.tr[r // 2, r % 2 : r % 2 + 1, :]
        if m < 10:
            K.tailx[5 + i : 6 + i, 128 * m : 128 * m + 128] = row
        else:
            K.tailb[5 + i : 6 + i, 128 * (m - 10) : 128 * (m - 10) + 128] = row

    def resp_bc(j):
        bc_forward(K.rbc, j, j + 1, lambda lanes: K.tailb[:, lanes])

    def resp_local(j, g):
        lanes = lanes_of(g)
        rows = rows_of(j)
        w = taps(K.cw, lanes)
        xc, gp = conv(K.rx[rows, lanes].astype(F32), K.tailx[:, lanes], w)
        z = K.rz[rows, lanes].astype(F32)
        live = jnp.where(iota((T, 128), 0) < K.rlen[0, j], z * sigmoid(z), 0.0)
        dy = K.rcot[rows, lanes].astype(F32) * live
        dt = K.dtE[rows_of(j + 1), lanes]
        yin, dxd, xdr, dyr = attend(j + 1, g, xc, dy, dt)
        K.acc[j + 1] += reduce_heads(g, dyr * yin - xdr * dxd, xc * dxd)
        gain = K.dex[:, lanes]
        K.yl[rows, lanes] = yin + gain * xc
        K.dD[:, lanes] += fold8(dy * xc)
        e = jnp.exp(cum_pair(j + 1, g))
        K.ee[rows, lanes] = e
        K.edy[rows, lanes] = (e * dy).astype(BF)
        dx = conv_back((dt * dxd + gain * dy) * gp, w, K.dw, lanes, K.dtailx)
        K.o_rdx[rows, lanes] = dx.astype(BF)

    def resp_range(lo, hi):
        def one(i):
            resp_local(i // NG, lax.rem(i, NG))

        pl.loop(lo, hi)(one)

    pl.loop(0, 4)(resp_bc)
    resp_range(0, NG)
    wait_all(f1)
    choose(K.of, K.fh, K.fl)
    f2 = spread(lambda p: K.fl.at[p], K.fr.at[me], 3)
    start_all(f2)
    K.fr[me] = K.fl[me]
    resp_range(NG, 4 * NG)

    def state_grad(g):
        lanes = lanes_of(g)
        K.dS[lanes, :] = mm(K.edy[:, lanes], K.Cb[1:5].reshape(4 * T, NS), 0, 0).astype(BF)

    pl.loop(0, NG)(state_grad)
    wait_all(f2)

    def gather_rows(ref, k):
        spot = pl.ds(pl.multiple_of(8 * k, 8), 8)
        return [jnp.concatenate([ref[2 * i + half, spot, :] for i in range(16)], axis=0) for half in range(2)]

    b_halves = gather_rows(K.fr, 5)
    bp = jnp.concatenate(b_halves, axis=1)
    bph, bpl = split2(bp)

    def back(k, dbp):
        halves = gather_rows(K.fr, k)
        for half in range(2):
            g = 5 * half + k
            lanes = lanes_of(g)
            xh, xl = split2(halves[half])
            K.S[lanes, :] = (mm(xh, bph, 0, 0) + mm(xh, bpl, 0, 0) + mm(xl, bph, 0, 0)).astype(BF)
            dSg = K.dS[lanes, :]
            u = mm(bph, dSg, 1, 1)
            dbp = dbp + mm(xh, dSg, 1, 0)
            spot = pl.ds(pl.multiple_of(8 * k, 8), 8)
            for i in range(16):
                K.bs[2 * i + half, spot, :] = u[8 * i : 8 * i + 8, :]
        return dbp

    dbp = lax.fori_loop(0, 5, back, jnp.zeros((T, NS), F32))
    for c in range(32):
        K.bs[c, 40:48, :] = dbp[8 * (c // 2) : 8 * (c // 2) + 8, 128 * (c % 2) : 128 * (c % 2) + 128]
    b1 = spread(lambda p: K.bs.at[p], K.bh.at[me], 4)
    start_all(b1)
    K.bh[me] = K.bs[me]

    def resp_state(i):
        j = i // NG
        g = lax.rem(i, NG)
        lanes = lanes_of(g)
        rows = rows_of(j)
        cs = mm(K.Cb[j + 1], K.S[lanes, :], 1, 1)
        z = K.rz[rows, lanes].astype(F32)
        y = K.yl[rows, lanes] + K.ee[rows, lanes] * cs
        K.o_out[rows, lanes] = (y * (z * sigmoid(z))).astype(BF)
        K.acc[j + 1] += reduce_heads(g, K.edy[rows, lanes].astype(F32) * cs)

    pl.loop(0, 4 * NG)(resp_state)

    def bc_back(bc_ref, at, q, tail, dc_more, db_more, o_ref, tail_ref):
        dgm = jnp.where(lower, K.dG[q], 0.0)
        dc = mm3(dgm, K.B[q], 1, 0) + dc_more
        db = mm3(dgm, K.C[q], 0, 0) + db_more
        for m in range(4):
            lanes = slice(128 * m, 128 * m + 128)
            d = db[:, lanes] if m < 2 else dc[:, 128 * (m - 2) : 128 * (m - 2) + 128]
            K.xs[0:8, :] = tail(lanes)
            K.xs[8:136, :] = bc_ref[rows_of(at), lanes].astype(F32)
            o_ref[rows_of(at), lanes] = conv_back(
                d * K.gpb[rows_of(q), lanes], taps(K.cbc, lanes), K.dwb, lanes, tail_ref
            )

    def resp_bc_back(j):
        more = mm(K.edy[rows_of(j), :], K.S[...], 1, 0)
        bc_back(K.rbc, j, j + 1, lambda lanes: K.tailb[:, lanes], more, 0.0, K.rsum, K.dtailb)

    pl.loop(0, 4)(resp_bc_back)

    K.us[...] = jnp.zeros((32, 2, 128), F32)
    for r in range(42):
        i, m = divmod(r, 14)
        if m < 10:
            row = K.dtailx[5 + i : 6 + i, 128 * m : 128 * m + 128]
        else:
            row = K.dtailb[5 + i : 6 + i, 128 * (m - 10) : 128 * (m - 10) + 128]
        K.us[r // 2, r % 2 : r % 2 + 1, :] = row
    u1 = spread(lambda p: K.us.at[p], K.uh.at[me], 5)
    start_all(u1)
    K.uh[me] = K.us[me]

    core = lax.rem(mt, 2)
    mate = mt + 1 - 2 * core
    across = lax.rem(mt + 2, 4)

    def tensor_copy(src, dst, at, peer):
        return pltpu.make_async_remote_copy(
            src_ref=src, dst_ref=dst, send_sem=K.tsem.at[at, 0], recv_sem=K.tsem.at[at, 1],
            device_id={"tensor": peer}, device_id_type=pl.DeviceIdType.MESH,
        )

    def tensor_sum(buf, recv, full, half, at):
        mine = pl.ds(pl.multiple_of(core * half, 8), half)
        other = pl.ds(pl.multiple_of((1 - core) * half, 8), half)
        steps = [
            tensor_copy(buf.at[other, :], recv.at[0], at, mate),
            tensor_copy(buf.at[mine, :], recv.at[1], at + 1, across),
            tensor_copy(buf.at[mine, :], full.at[mine, :], at + 2, mate),
        ]

        def add(slot):
            def one(i):
                spot = pl.ds(pl.multiple_of(core * half + i * 8, 8), 8)
                buf[spot, :] += recv[slot, pl.ds(pl.multiple_of(i * 8, 8), 8), :]

            pl.loop(0, half // 8)(one)

        def keep():
            if n == 1:
                full[...] = buf[...]
            else:
                full[mine, :] = buf[mine, :]

        return steps, add, keep

    rsteps, radd, rkeep = tensor_sum(K.rsum, K.rrecv, K.o_rdbc, 256, 0)
    if n > 1:
        rsteps[0].start()

    wait_all(b1)
    choose(K.inv, K.bh, K.bl)
    b2 = spread(lambda p: K.bl.at[p], K.br.at[me], 6)
    start_all(b2)
    K.br[me] = K.bl[me]
    wait_all(u1)
    choose(K.inv, K.uh, K.ul)
    u2 = spread(lambda p: K.ul.at[p], K.ur.at[me], 7)
    start_all(u2)
    K.ur[me] = K.ul[me]

    if n > 1:
        rsteps[0].wait()
        radd(0)
        rsteps[1].start()

    pl.loop(0, NG)(prompt_local)

    def steps_back(q, at, o_ref, extra):
        a = K.acc[q].T
        dlr = mmx(a[0:NH, :], trir, 1, 0)
        if extra:
            dlr = dlr + mmx(K.accq[...].T[0:NH, :], tris, 1, 0)
        draw = (a[32 : 32 + NH, :] + K.col[0] * dlr) * K.sig[q]
        o_ref[:, pl.ds(pl.multiple_of(at * T, T), T)] = draw
        K.dlr[...] += K.lr[q] * dlr
        K.ddr[...] += draw

    pl.loop(0, 4)(lambda j: steps_back(j + 1, j, K.o_rddt, False))
    wait_all(b2)
    wait_all(u2)
    if n > 1:
        rsteps[1].wait()
        radd(1)
        rsteps[2].start()
    rkeep()

    for r in range(42):
        i, m = divmod(r, 14)
        row = K.ur[r // 2, r % 2 : r % 2 + 1, :]
        if m < 10:
            K.dtailx[5 + i : 6 + i, 128 * m : 128 * m + 128] = row
        else:
            K.dtailb[5 + i : 6 + i, 128 * (m - 10) : 128 * (m - 10) + 128] = row

    def prompt_final(k):
        halves = gather_rows(K.br, k)
        for half in range(2):
            g = 5 * half + k
            lanes = lanes_of(g)
            w = taps(K.cw, lanes)
            cum = cum_pair(0, g)
            lu = jnp.exp(cum[T - 1 : T, :] - cum) * halves[half]
            dt = K.dtE[0:T, lanes]
            xc = K.pxc[:, lanes]
            xlu = xc * lu
            K.accq[...] += reduce_heads(g, dt * xlu)
            K.acc[0] += reduce_heads(g, jnp.zeros_like(xlu), xlu)
            dxd = K.pdxd[:, lanes] + lu
            dv = (dt * dxd + K.dex[:, lanes] * K.pdy[:, lanes]) * K.pgp[:, lanes]
            K.xs[0:8, :] = jnp.zeros((8, 128), F32)
            K.xs[8:136, :] = K.px[:, lanes].astype(F32)
            dx = conv_back(dv, w, K.dw, lanes, None)
            K.ds[8:136, :] = dx
            K.ds[128:136, :] += K.dtailx[:, lanes]
            K.o_pdx[:, lanes] = K.ds[8:136, :].astype(BF)

    pl.loop(0, 5)(prompt_final)
    db_more = jnp.concatenate(gather_rows(K.br, 5), axis=1)
    bc_back(K.pbc, 0, 0, lambda lanes: jnp.zeros((8, 128), F32), 0.0, db_more, K.psum, None)
    K.psum[120:128, :] += K.dtailb[...]
    K.psum[128:144, :] = jnp.zeros((16, BCW), F32)
    for k in range(4):
        K.psum[128 + k : 129 + k, :] = jnp.sum(K.dwb[k], axis=0, keepdims=True)
    psteps, padd, pkeep = tensor_sum(K.psum, K.precv, K.pfull, 72, 3)
    if n > 1:
        psteps[0].start()
    steps_back(0, 0, K.o_pddt, True)
    if n > 1:
        psteps[0].wait()
        padd(0)
        psteps[1].start()

    K.ps[...] = jnp.zeros((32, 2, 128), F32)

    def put(r, row):
        K.ps[r // 2, r % 2 : r % 2 + 1, :] = row

    for k in range(4):
        total = jnp.sum(K.dw[k], axis=0, keepdims=True)
        for g in range(NG):
            put(k * NG + g, total[:, 128 * g : 128 * g + 128])
    skip = jnp.zeros((8, 128), F32)
    for g in range(NG):
        skip = skip + mm(jnp.concatenate(split2(K.dD[:, 128 * g : 128 * g + 128]), axis=1), K.R[g, :256, :], 1, 0)
    spread_eye = iota((NH, 128), 0) == iota((NH, 128), 1)

    def as_row(ref):
        total = jnp.sum(ref[...], axis=1, keepdims=True)
        return jnp.sum(jnp.where(spread_eye, jnp.broadcast_to(total, (NH, 128)), 0.0), axis=0, keepdims=True)

    put(56, as_row(K.dlr))
    put(57, as_row(K.ddr))
    put(58, jnp.sum(skip, axis=0, keepdims=True))
    if n > 1:
        rsteps[2].wait()
        psteps[1].wait()
        padd(1)
        psteps[2].start()
        psteps[2].wait()
    pkeep()
    for k in range(4):
        for m in range(4):
            put(40 + 4 * k + m, K.pfull[128 + k : 129 + k, 128 * m : 128 * m + 128])
    K.o_pdbc[...] = K.pfull[0:128, :]
    if n > 1:
        p1 = spread(lambda p: K.ps.at[p], K.ph.at[me], 0)
        start_all(p1)
        K.ph[me] = K.ps[me]
        wait_all(p1)
        K.pr[me] = jnp.sum(K.ph[...], axis=0)
        p2 = spread(lambda p: K.pr.at[me], K.pr.at[me], 1)
        start_all(p2)
        wait_all(p2)
    else:
        K.pr[...] = K.ps[...]
    for k in range(4):
        for g in range(NG):
            r = k * NG + g
            K.o_cw[k : k + 1, 128 * g : 128 * g + 128] = K.pr[r // 2, r % 2 : r % 2 + 1, :]
        for m in range(4):
            r = 40 + 4 * k + m
            K.o_cbc[k : k + 1, 128 * m : 128 * m + 128] = K.pr[r // 2, r % 2 : r % 2 + 1, :]
    for i in range(3):
        r = 56 + i
        K.o_hp[i : i + 1, :] = K.pr[r // 2, r % 2 : r % 2 + 1, 0:NH]


def body(n, nt, *args):
    (px, pbc, pdt, pz, rx, rbc, rdt, rz, cw, cbc, hp, of, rlen, pcot, rcot) = args
    inv = jnp.sum(
        jnp.where(of[:, None] == jnp.arange(n)[None, :], jnp.arange(n, dtype=jnp.int32)[:, None], 0), axis=0
    ).astype(jnp.int32)
    table = scratch_table(32)
    vm = pl.BlockSpec(memory_space=pltpu.VMEM)
    sm = pl.BlockSpec(memory_space=pltpu.SMEM)
    shape = jax.ShapeDtypeStruct
    if n == 1:
        of = jnp.arange(32, dtype=jnp.int32)
        inv = of
    params = dict(vmem_limit_bytes=60 * 1024 * 1024, has_side_effects=True)
    if n > 1:
        params["collective_id"] = 0
    return pl.pallas_call(
        functools.partial(kernel, n, nt),
        out_shape=(
            shape((512, CHD), BF), shape((T, CHD), BF), shape((T, BCW), F32), shape((NH, T), F32),
            shape((512, CHD), BF), shape((512, BCW), F32), shape((NH, 512), F32),
            shape((4, CHD), F32), shape((4, BCW), F32), shape((3, NH), F32),
        ),
        in_specs=[vm] * 13 + [sm] * 3,
        out_specs=[vm] * 10,
        scratch_shapes=list(table.values()),
        compiler_params=pltpu.CompilerParams(**params),
    )(px, pbc, pdt, pz, pcot, rx, rbc, rdt, rz, rcot, cw, cbc, hp, of, inv, rlen)


def solution(mesh):
    n = mesh.shape["dp"]
    nt = mesh.shape["tensor"]
    placed = (
        P("dp", "tensor"), P("dp", None), P("tensor", "dp"), P("dp", "tensor"),
        P("dp", "tensor"), P("dp", None), P("tensor", "dp"), P("dp", "tensor"),
        P(None, "tensor"), P(), P(None, "tensor"), P(), P("dp", None),
        P("dp", "tensor"), P("dp", "tensor"),
    )
    return jax.shard_map(
        functools.partial(body, n, nt),
        mesh=mesh,
        in_specs=placed,
        out_specs=(
            P("dp", "tensor"), P("dp", "tensor"), P("dp", None), P("tensor", "dp"),
            P("dp", "tensor"), P("dp", None), P("tensor", "dp"),
            P(None, "tensor"), P(), P(None, "tensor"),
        ),
        check_vma=False,
    )
```

```python
import functools
import types

import jax
import jax.numpy as jnp
from jax import lax
from jax.experimental import pallas as pl
from jax.experimental.pallas import tpu as pltpu
from jax.sharding import PartitionSpec as P

F32 = jnp.float32
BF = jnp.bfloat16
T = 128
NH = 20
NG = 10
NS = 256
CHD = 1280
BCW = 512
UNROLL = 5
ROW = 40
SMALL = 10


def mm(a, b, ca, cb):
    return lax.dot_general(a, b, (((ca,), (cb,)), ((), ())), preferred_element_type=F32)


def split2(a):
    hi = a.astype(BF)
    return hi, (a - hi.astype(F32)).astype(BF)


def split3(a):
    hi = a.astype(BF)
    rest = a - hi.astype(F32)
    mid = rest.astype(BF)
    return hi, mid, (rest - mid.astype(F32)).astype(BF)


def mm3(a, b, ca, cb):
    ah, al = split2(a)
    bh, bl = split2(b)
    return mm(ah, bh, ca, cb) + mm(ah, bl, ca, cb) + mm(al, bh, ca, cb)


def mmx(a, ones, ca, cb):
    hi, mid, lo = split3(a)
    return mm(hi, ones, ca, cb) + mm(mid, ones, ca, cb) + mm(lo, ones, ca, cb)


def sigmoid(v):
    return 0.5 + 0.5 * jnp.tanh(0.5 * v)


def softplus(u):
    e = jnp.exp(-jnp.abs(u))
    s = e / (2.0 + e)
    q = s * s
    poly = 1.0 + q * (1 / 3 + q * (1 / 5 + q * (1 / 7 + q * (1 / 9 + q * (1 / 11 + q / 13)))))
    return jnp.maximum(u, 0.0) + 2.0 * s * poly


def iota(shape, dim):
    return lax.broadcasted_iota(jnp.int32, shape, dim)


def fold8(a):
    return jnp.sum(a.reshape(16, 8, 128), axis=0)


BIG_IN = ("px", "pbc", "pz", "pcot", "rx", "rbc", "rz", "rcot")
SMALL_IN = ("pdt", "rdt", "cw", "cbc", "hp")
SCALARS = ("of", "rlen")
BIG_OUT = ("out", "pdx", "rdx", "rdbc")
SMALL_OUT = ("o_pdbc", "o_pddt", "o_rddt", "o_cw", "o_cbc", "o_hp")
SHAPES = dict(
    px=((T, CHD), BF), pbc=((T, BCW), BF), pz=((T, CHD), BF), pcot=((T, CHD), BF),
    rx=((512, CHD), BF), rbc=((512, BCW), BF), rz=((512, CHD), BF), rcot=((512, CHD), BF),
    out=((512, CHD), BF), pdx=((T, CHD), BF), rdx=((512, CHD), BF), rdbc=((512, BCW), F32),
)


def scratch_table():
    v = pltpu.VMEM
    dma = pltpu.SemaphoreType.DMA
    table = {name: v(*SHAPES[name]) for name in BIG_IN + BIG_OUT}
    for one in "tfbve":
        rows = {"t": SMALL, "f": ROW, "b": ROW, "v": 8, "e": 2}[one]
        for part in "shlr":
            table[one + part] = v((32, rows, 128), F32)
    table.update(
        hp_sum=v((4, 64, 128), F32), hp_in=v((3, 4, 64, 128), F32), cb_in=v((4, 32, 128), F32), cb_out=v((32, 128), F32),
        rsum=v((512, BCW), F32), rrecv=v((4, 2, 64, BCW), F32),
        psum=v((T, BCW), F32), pfull=v((T, BCW), F32), precv=v((2, 64, BCW), F32),
        invv=v((1, 128), jnp.int32), inv=pltpu.SMEM((1, 128), jnp.int32),
        adt=v((NH, T), F32),
        dtr=v((6, NH, T), F32), sig=v((6, NH, T), F32), lr=v((6, NH, T), F32), cumr=v((6, NH, T), F32),
        tmp=v((6, 128, 128), F32), col=v((2, NH, 1), F32), dex=v((1, CHD), F32),
        cumB=v((6 * NH, T, T), F32), dtE=v((6 * T, CHD), F32),
        R=v((NG, 512, 128), BF),
        B=v((6, T, NS), F32), C=v((5, T, NS), F32), Cb=v((5, T, NS), BF), gpb=v((6 * T, BCW), F32),
        G=v((5, T, T), F32), dG=v((5, T, T), F32), acc=v((6, T, 128), F32), accq=v((T, 128), F32),
        xs=v((5, 136, 128), F32), ds=v((5, 144, 128), F32),
        tailx=v((8, CHD), F32), tailb=v((8, BCW), F32), dtailx=v((8, CHD), F32), dtailb=v((8, BCW), F32),
        dw=v((4, 8, CHD), F32), dwb=v((4, 8, BCW), F32), dD=v((8, CHD), F32),
        pxc=v((T, CHD), F32), pgp=v((T, CHD), F32), pdxf=v((T, CHD), F32),
        live=v((512, 128), F32), dy=v((512, CHD), F32), sz=v((512, CHD), F32),
        yl=v((T, CHD), F32), edy=v((512, CHD), BF), ee=v((512, CHD), F32),
        S=v((CHD, NS), BF), dS=v((CHD, NS), BF),
        dlr=v((NH, T), F32), ddr=v((NH, T), F32),
        sem=dma((10, 2, 32)), tsem=dma((16, 2)), gsem=dma((4, 2, 4)), isem=dma((len(BIG_IN) + 1,)), osem=dma((len(BIG_OUT) + 3,)),
    )
    return table


def kernel(n, nt, *refs):
    names = [name + "_in" for name in BIG_IN] + list(SMALL_IN) + list(SCALARS)
    names += [name + "_out" for name in BIG_OUT] + list(SMALL_OUT) + list(scratch_table())
    K = types.SimpleNamespace(**dict(zip(names, refs)))
    me = lax.axis_index("dp")
    mt = lax.axis_index("tensor")
    left = iota((T, 128), 1) < 64
    lower = iota((T, T), 0) >= iota((T, T), 1)
    mesh_ids = pl.DeviceIdType.MESH
    many = n > 1

    if many:
        barrier = pltpu.get_barrier_semaphore()

        def greet(k):
            pl.semaphore_signal(barrier, inc=1, device_id={"dp": lax.rem(me + k, n)}, device_id_type=mesh_ids)

        pl.loop(1, n)(greet)
        for k in range(1, nt):
            pl.semaphore_signal(barrier, inc=1, device_id={"tensor": lax.rem(mt + k, nt)}, device_id_type=mesh_ids)

    loads = {
        name: pltpu.make_async_copy(getattr(K, name + "_in"), getattr(K, name), K.isem.at[i])
        for i, name in enumerate(BIG_IN)
    }
    for name in BIG_IN:
        loads[name].start()

    class Relay:
        def __init__(self, key, sem, table):
            self.s, self.h, self.l, self.r = (getattr(K, key + part) for part in "shlr")
            self.sem = sem
            self.table = table

        def copy(self, src, dst, sem):
            def one(k):
                peer = lax.rem(me + k, n)
                return pltpu.make_async_remote_copy(
                    src_ref=src.at[peer], dst_ref=dst.at[me], send_sem=K.sem.at[sem, 0, k], recv_sem=K.sem.at[sem, 1, k],
                    device_id={"dp": peer}, device_id_type=mesh_ids,
                )

            return one

        def send(self):
            if many:
                one = self.copy(self.s, self.h, self.sem)
                pl.loop(1, n)(lambda k: one(k).start())
                self.h[me] = self.s[me]

        def turn(self):
            if many:
                one = self.copy(self.s, self.h, self.sem)
                pl.loop(1, n)(lambda k: one(k).wait())

                def pick(d):
                    self.l[d] = self.h[self.table(d)]

                pl.loop(0, n)(pick)
                two = self.copy(self.l, self.r, self.sem + 1)
                pl.loop(1, n)(lambda k: two(k).start())
                self.r[me] = self.l[me]

        def end(self):
            if many:
                two = self.copy(self.l, self.r, self.sem + 1)
                pl.loop(1, n)(lambda k: two(k).wait())
            else:
                self.r[...] = self.s[...]

    forth = lambda d: K.of[d]
    home = lambda d: K.inv[0, d]
    rt, rf = Relay("t", 0, forth), Relay("f", 2, forth)
    rb, rd, re = Relay("b", 4, home), Relay("v", 6, home), Relay("e", 8, home)

    def lanes_of(g):
        return pl.ds(pl.multiple_of(g * 128, 128), 128)

    def rows_of(q):
        return pl.ds(pl.multiple_of(q * T, T), T)

    def scatter_rows(ref, k, half, tile):
        spot = pl.ds(pl.multiple_of(8 * k, 8), 8)
        for i in range(16):
            ref[2 * i + half, spot, :] = tile[8 * i : 8 * i + 8, :]

    def gather_rows(ref, k, half):
        spot = pl.ds(pl.multiple_of(8 * k, 8), 8)
        return jnp.concatenate([ref[2 * i + half, spot, :] for i in range(16)], axis=0)

    def tail_rows(rows_x, rows_b):
        for r in range(42):
            i, m = divmod(r, 14)
            ref, m = (rows_x, m) if m < 10 else (rows_b, m - 10)
            yield r, ref, slice(5 + i, 6 + i), slice(128 * m, 128 * m + 128)

    loads["px"].wait()
    loads["pbc"].wait()
    K.tailx[...] = K.px[112:128, :].astype(F32)[8:16, :]
    K.tailb[...] = K.pbc[112:128, :].astype(F32)[8:16, :]
    K.ts[:, 8:10, :] = jnp.zeros((32, 2, 128), F32)
    for r, ref, row, lanes in tail_rows(K.tailx, K.tailb):
        K.ts[r // 2, 8 + r % 2 : 9 + r % 2, :] = ref[row, lanes]
    for h in range(NH):
        r = 42 + h
        K.ts[r // 2, 8 + r % 2 : 9 + r % 2, :] = K.pdt[h : h + 1, :]
    for half in range(2):
        scatter_rows(K.ts, 0, half, K.pbc[:, 128 * half : 128 * half + 128].astype(F32))

    def pack_x(k):
        for half in range(2):
            scatter_rows(K.fs, k, half, K.px[:, lanes_of(5 * half + k)].astype(F32))

    if many:
        pl.semaphore_wait(barrier, n - 1 + nt - 1)
    rt.send()
    pl.loop(0, 5)(pack_x)
    rf.send()

    tri = (iota((T, T), 0) <= iota((T, T), 1)).astype(F32).astype(BF)
    trir = (iota((T, T), 0) >= iota((T, T), 1)).astype(F32).astype(BF)
    tris = (iota((T, T), 0) < iota((T, T), 1)).astype(F32).astype(BF)
    eye = iota((NH, NH), 0) == iota((NH, NH), 1)

    lane = iota((1, 128), 1)
    back_to = jnp.zeros((1, 128), jnp.int32)
    for d in range(n):
        back_to = jnp.where(lane == K.of[d], d, back_to)
    K.invv[...] = back_to
    inv_copy = pltpu.make_async_copy(K.invv, K.inv, K.isem.at[len(BIG_IN)])
    inv_copy.start()

    def column(row):
        return jnp.sum(jnp.where(eye, jnp.broadcast_to(K.hp[row : row + 1, :], (NH, NH)), 0.0), axis=1, keepdims=True)

    K.col[0] = -jnp.exp(column(0))
    K.col[1] = column(1)
    for g in range(NG):
        K.dex[:, 128 * g : 128 * g + 128] = jnp.where(
            lane < 64, K.hp[2:3, 2 * g : 2 * g + 1], K.hp[2:3, 2 * g + 1 : 2 * g + 2]
        )
    for j in range(4):
        K.live[j * T : j * T + T, :] = jnp.where(iota((T, 128), 0) < K.rlen[0, j], 1.0, 0.0)

    def make_R(g):
        r = iota((512, 128), 0)
        want = 2 * g + jnp.where((r & 127) >= 64, 1, 0) + jnp.where(r >= 256, 32, 0)
        K.R[g] = (iota((512, 128), 1) == want).astype(F32).astype(BF)

    pl.loop(0, NG)(make_R)
    for name in ("dG", "acc", "accq", "dw", "dwb", "dD", "dtailx", "dtailb", "dlr", "ddr", "ds", "tmp"):
        ref = getattr(K, name)
        ref[...] = jnp.zeros(ref.shape, F32)

    def step_tables(dt_ref, ats, qs):
        every = list(zip(ats, qs))
        for at, q in every:
            u = dt_ref[:, at * T : at * T + T] + K.col[1]
            dt = softplus(u)
            lr = K.col[0] * dt
            cum = mmx(lr, tri, 1, 0)
            K.sig[q] = 1.0 / (1.0 + jnp.exp(-u))
            K.lr[q] = lr
            K.cumr[q] = cum
            K.tmp[q, 0:NH, :] = cum
            K.tmp[q, 32 : 32 + NH, :] = dt
        for at, q in every:
            cols = K.tmp[q].T
            for h in range(NH):
                K.cumB[q * NH + h] = jnp.broadcast_to(cols[:, h : h + 1], (T, T))
            for g in range(NG):
                a = 32 + 2 * g
                K.dtE[q * T : q * T + T, 128 * g : 128 * g + 128] = jnp.where(
                    left, jnp.broadcast_to(cols[:, a : a + 1], (T, 128)), jnp.broadcast_to(cols[:, a + 1 : a + 2], (T, 128))
                )

    def conv(x, tail, w, u=0):
        K.xs[u, 0:8, :] = tail
        K.xs[u, 8:136, :] = x
        v = w[0] * K.xs[u, 5:133, :] + w[1] * K.xs[u, 6:134, :] + w[2] * K.xs[u, 7:135, :] + w[3] * x
        s = sigmoid(v)
        xc = v * s
        return xc, s + xc * (1.0 - s)

    def conv_taps(dv, dw_ref, lanes, u=0):
        for k in range(4):
            dw_ref[k, :, lanes] += fold8(dv * K.xs[u, 5 + k : 133 + k, :])

    def conv_back(dv, w, tail_ref=None, lanes=None, u=0):
        K.ds[u, 8:136, :] = dv
        if tail_ref is not None:
            tail_ref[:, lanes] += w[0] * K.ds[u, 3:11, :] + w[1] * K.ds[u, 2:10, :] + w[2] * K.ds[u, 1:9, :]
        return w[3] * dv + w[2] * K.ds[u, 9:137, :] + w[1] * K.ds[u, 10:138, :] + w[0] * K.ds[u, 11:139, :]

    def taps(ref, lanes):
        return [ref[k : k + 1, lanes] for k in range(4)]

    no_tail = jnp.zeros((8, 128), F32)

    def bc_forward(bc_ref, at, q, tail, u=0):
        for m in range(4):
            lanes = slice(128 * m, 128 * m + 128)
            xc, gp = conv(bc_ref[rows_of(at), lanes].astype(F32), tail(lanes), taps(K.cbc, lanes), m)
            K.gpb[rows_of(q), lanes] = gp
            if m < 2:
                K.B[q, :, lanes] = xc
            else:
                half = slice(128 * (m - 2), 128 * (m - 2) + 128)
                K.C[q, :, half] = xc
                K.Cb[q, :, half] = xc.astype(BF)
        K.G[q] = jnp.where(lower, mm3(K.C[q], K.B[q], 1, 1), 0.0)

    def bc_back(bc_ref, at, q, tail, dc_more, o_ref, tail_ref):
        dgm = jnp.where(lower, K.dG[q], 0.0)
        dc = mm3(dgm, K.B[q], 1, 0) + dc_more
        db = mm3(dgm, K.C[q], 0, 0)
        for m in range(4):
            lanes = slice(128 * m, 128 * m + 128)
            d = db[:, lanes] if m < 2 else dc[:, 128 * (m - 2) : 128 * (m - 2) + 128]
            dv = d * K.gpb[rows_of(q), lanes]
            K.xs[m, 0:8, :] = tail(lanes)
            K.xs[m, 8:136, :] = bc_ref[rows_of(at), lanes].astype(F32)
            conv_taps(dv, K.dwb, lanes, m)
            o_ref[rows_of(at), lanes] = conv_back(dv, taps(K.cbc, lanes), tail_ref, lanes, m)

    def cum_pair(q, g):
        return jnp.where(left, K.cumB[q * NH + 2 * g], K.cumB[q * NH + 2 * g + 1])

    def attend(q, g, xc, dy, dt):
        xd = dt * xc
        x2 = jnp.concatenate([jnp.where(left, xd, 0.0).astype(BF), jnp.where(left, 0.0, xd).astype(BF)], axis=0)
        d2 = jnp.concatenate([jnp.where(left, dy, 0.0).astype(BF), jnp.where(left, 0.0, dy).astype(BF)], axis=0)
        xdb = xd.astype(BF)
        dyb = dy.astype(BF)
        scores = K.G[q]
        decay = [
            jnp.exp(jnp.minimum(K.cumB[q * NH + 2 * g + i] - K.cumr[q, pl.ds(2 * g + i, 1), :], 0.0)) for i in range(2)
        ]
        mix = [(scores * one).astype(BF) for one in decay]
        yin = mm(jnp.concatenate(mix, axis=1), x2, 1, 0)
        dxd = mm(jnp.concatenate(mix, axis=0), d2, 0, 0)
        dmix = mm(dyb, x2, 1, 1)
        K.dG[q] += dmix[:, :T] * decay[0] + dmix[:, T:] * decay[1]
        return yin, dxd, xdb.astype(F32), dyb.astype(F32)

    def reduce_heads(g, first, second=None):
        parts = list(split2(first))
        if second is not None:
            parts += split2(second)
        return mm(jnp.concatenate(parts, axis=1), K.R[g, : 128 * len(parts), :], 1, 0)

    def steps_back(q, o_ref, at):
        a = K.acc[q].T
        dlr = mmx(a[0:NH, :], trir, 1, 0)
        draw = (a[32 : 32 + NH, :] + K.col[0] * dlr) * K.sig[q]
        o_ref[:, pl.ds(pl.multiple_of(at * T, T), T)] = draw
        K.dlr[...] += K.lr[q] * dlr
        K.ddr[...] += draw

    def state_steps(acc, q):
        a = acc[...].T
        dlr = mmx(a[0:NH, :], tris, 1, 0)
        return dlr, (a[32 : 32 + NH, :] + K.col[0] * dlr) * K.sig[q]

    step_tables(K.pdt, [0], [0])
    bc_forward(K.pbc, 0, 0, lambda lanes: no_tail)
    loads["pz"].wait()
    loads["pcot"].wait()

    def prompt_local(i):
        for u in range(UNROLL):
            g = i * UNROLL + u
            lanes = lanes_of(g)
            w = taps(K.cw, lanes)
            xc, gp = conv(K.px[:, lanes].astype(F32), no_tail, w, u)
            K.pxc[:, lanes] = xc
            K.pgp[:, lanes] = gp
            z = K.pz[:, lanes].astype(F32)
            dy = K.pcot[:, lanes].astype(F32) * (z * sigmoid(z))
            dt = K.dtE[0:T, lanes]
            yin, dxd, xdr, dyr = attend(0, g, xc, dy, dt)
            K.acc[0] += reduce_heads(g, dyr * yin - xdr * dxd, xc * dxd)
            K.dD[:, lanes] += fold8(dy * xc)
            dv = (dt * dxd + K.dex[:, lanes] * dy) * gp
            conv_taps(dv, K.dw, lanes, u)
            K.pdxf[:, lanes] = conv_back(dv, w, u=u)

    pl.loop(0, NG // UNROLL)(prompt_local)
    bc_back(K.pbc, 0, 0, lambda lanes: no_tail, 0.0, K.psum, None)
    steps_back(0, K.o_pddt, 0)

    rt.turn()

    step_tables(K.rdt, [0, 1, 2, 3], [1, 2, 3, 4])
    loads["rz"].wait()
    loads["rcot"].wait()

    def gates(i):
        j = i // NG
        g = lax.rem(i, NG)
        lanes = lanes_of(g)
        rows = rows_of(j)
        z = K.rz[rows, lanes].astype(F32)
        sz = z * sigmoid(z)
        dy = K.rcot[rows, lanes].astype(F32) * (sz * K.live[rows, :])
        e = jnp.exp(cum_pair(j + 1, g))
        K.sz[rows, lanes] = sz
        K.dy[rows, lanes] = dy
        K.ee[rows, lanes] = e
        K.edy[rows, lanes] = (e * dy).astype(BF)

    pl.loop(0, 4 * NG, unroll=2)(gates)
    rf.turn()
    loads["rx"].wait()
    loads["rbc"].wait()
    inv_copy.wait()
    rt.end()

    for r, ref, row, lanes in tail_rows(K.tailx, K.tailb):
        ref[row, lanes] = K.tr[r // 2, 8 + r % 2 : 9 + r % 2, :]
    for h in range(NH):
        r = 42 + h
        K.adt[h : h + 1, :] = K.tr[r // 2, 8 + r % 2 : 9 + r % 2, :]
    for j in range(4):
        bc_forward(K.rbc, j, j + 1, lambda lanes: K.tailb[:, lanes])
    for half in range(2):
        lanes = slice(128 * half, 128 * half + 128)
        xc, gp = conv(gather_rows(K.tr, 0, half), no_tail, taps(K.cbc, lanes), half)
        K.B[5, :, lanes] = xc
        K.gpb[5 * T : 6 * T, lanes] = gp

    def state_grad(k):
        bh = K.B[5].astype(BF)
        for half in range(2):
            lanes = lanes_of(5 * half + k)
            ds = mm(K.edy[:, lanes], K.Cb[1:5].reshape(4 * T, NS), 0, 0).astype(BF)
            K.dS[lanes, :] = ds
            scatter_rows(K.bs, k, half, mm(bh, ds, 1, 1))

    pl.loop(0, 5)(state_grad)
    rb.send()
    step_tables(K.adt, [0], [5])

    def resp_local(j, with_state):
        def five(i):
            for u in range(UNROLL):
                g = i * UNROLL + u
                lanes = lanes_of(g)
                rows = rows_of(j)
                w = taps(K.cw, lanes)
                xc, gp = conv(K.rx[rows, lanes].astype(F32), K.tailx[:, lanes], w, u)
                dy = K.dy[rows, lanes]
                dt = K.dtE[rows_of(j + 1), lanes]
                yin, dxd, xdr, dyr = attend(j + 1, g, xc, dy, dt)
                gain = K.dex[:, lanes]
                y = yin + gain * xc
                steps = dyr * yin - xdr * dxd
                if with_state:
                    cs = mm(K.Cb[j + 1], K.S[lanes, :], 1, 1)
                    K.out[rows, lanes] = ((y + K.ee[rows, lanes] * cs) * K.sz[rows, lanes]).astype(BF)
                    steps = steps + K.edy[rows, lanes].astype(F32) * cs
                else:
                    K.yl[rows, lanes] = y
                K.acc[j + 1] += reduce_heads(g, steps, xc * dxd)
                K.dD[:, lanes] += fold8(dy * xc)
                dv = (dt * dxd + gain * dy) * gp
                conv_taps(dv, K.dw, lanes, u)
                K.rdx[rows, lanes] = conv_back(dv, w, K.dtailx, lanes, u).astype(BF)

        pl.loop(0, NG // UNROLL)(five)

    def resp_state(j):
        def five(i):
            for u in range(UNROLL):
                g = i * UNROLL + u
                lanes = lanes_of(g)
                rows = rows_of(j)
                cs = mm(K.Cb[j + 1], K.S[lanes, :], 1, 1)
                K.out[rows, lanes] = ((K.yl[rows, lanes] + K.ee[rows, lanes] * cs) * K.sz[rows, lanes]).astype(BF)
                K.acc[j + 1] += reduce_heads(g, K.edy[rows, lanes].astype(F32) * cs)

        pl.loop(0, NG // UNROLL)(five)

    def resp_bc_back(j):
        more = mm(K.edy[rows_of(j), :], K.S[...], 1, 0)
        bc_back(K.rbc, j, j + 1, lambda lanes: K.tailb[:, lanes], more, K.rsum, K.dtailb)

    core = lax.rem(mt, 2)
    mate = mt + 1 - 2 * core
    across = lax.rem(mt + 2, 4)

    class TensorSum:
        def __init__(self, buf, full, recv, base, at):
            mine = pl.ds(pl.multiple_of(base + core * 64, 8), 64)
            other = pl.ds(pl.multiple_of(base + (1 - core) * 64, 8), 64)
            self.buf, self.full, self.recv, self.base, self.mine = buf, full, recv, base, mine
            plan = ((buf.at[other, :], recv.at[0], mate), (buf.at[mine, :], recv.at[1], across),
                    (buf.at[mine, :], full.at[mine, :], mate))
            self.steps = [
                pltpu.make_async_remote_copy(
                    src_ref=src, dst_ref=dst, send_sem=K.tsem.at[at + i, 0], recv_sem=K.tsem.at[at + i, 1],
                    device_id={"tensor": peer}, device_id_type=mesh_ids,
                )
                for i, (src, dst, peer) in enumerate(plan)
            ] if many else None

        def go(self, stage):
            if not many:
                if stage == 0:
                    rows = pl.ds(self.base, T)
                    self.full[rows, :] = self.buf[rows, :]
                return
            if stage > 0:
                self.steps[stage - 1].wait()
            if stage in (1, 2):
                self.buf[self.mine, :] += self.recv[stage - 1]
            if stage == 2:
                self.full[self.mine, :] = self.buf[self.mine, :]
            if stage < 3:
                self.steps[stage].start()

    sums = [TensorSum(K.rsum, K.rdbc, K.rrecv.at[j], j * T, 3 * j) for j in range(4)]

    resp_local(0, False)
    rf.end()

    def adopt(k, dbp):
        bh, bl = split2(K.B[5])
        for half in range(2):
            g = 5 * half + k
            lanes = lanes_of(g)
            xc, gp = conv(gather_rows(K.fr, k, half), no_tail, taps(K.cw, lanes), half)
            cum = cum_pair(5, g)
            lv = jnp.exp(cum[T - 1 : T, :] - cum)
            dt = K.dtE[5 * T : 6 * T, lanes]
            xd = dt * xc
            xh, xl = split2(lv * xd)
            K.S[lanes, :] = (mm(xh, bh, 0, 0) + mm(xh, bl, 0, 0) + mm(xl, bh, 0, 0)).astype(BF)
            dbp = dbp + mm(xh, K.dS[lanes, :], 1, 0)
            lu = lv * gather_rows(K.bs, k, half)
            K.acc[5] += reduce_heads(g, xd * lu, xc * lu)
            conv_taps(dt * lu * gp, K.dw, lanes, half)
        return dbp

    dbp = lax.fori_loop(0, 5, adopt, jnp.zeros((T, NS), F32))
    for half in range(2):
        lanes = slice(128 * half, 128 * half + 128)
        scatter_rows(K.vs, 0, half, dbp[:, lanes])
        K.xs[half, 0:8, :] = no_tail
        K.xs[half, 8:136, :] = gather_rows(K.tr, 0, half)
        conv_taps(dbp[:, lanes] * K.gpb[5 * T : 6 * T, lanes], K.dwb, lanes, half)
    rd.send()
    dlr, draw = state_steps(K.acc.at[5], 5)
    K.dlr[...] += K.lr[5] * dlr
    K.ddr[...] += draw

    resp_state(0)
    resp_local(1, True)
    resp_bc_back(0)
    sums[0].go(0)
    rb.turn()
    resp_bc_back(1)
    sums[0].go(1)
    sums[1].go(0)
    resp_local(2, True)
    resp_bc_back(2)
    sums[0].go(2)
    sums[1].go(1)
    sums[2].go(0)
    rd.turn()
    resp_local(3, True)
    store_rdx = pltpu.make_async_copy(K.rdx, K.rdx_out, K.osem.at[0])
    store_rdx.start()
    store_out = pltpu.make_async_copy(K.out, K.out_out, K.osem.at[1])
    store_out.start()
    resp_bc_back(3)
    sums[3].go(0)
    sums[1].go(2)
    sums[2].go(1)

    K.es[...] = jnp.zeros((32, 2, 128), F32)
    for r, ref, row, lanes in tail_rows(K.dtailx, K.dtailb):
        K.es[r // 2, r % 2 : r % 2 + 1, :] = ref[row, lanes]
    re.send()

    for j in range(4):
        steps_back(j + 1, K.o_rddt, j)
    K.hp_sum[0] = jnp.zeros((64, 128), F32)
    for k in range(4):
        total = jnp.sum(K.dw[k], axis=0, keepdims=True)
        for g in range(NG):
            K.hp_sum[0, k * NG + g : k * NG + g + 1, :] = total[:, 128 * g : 128 * g + 128]
        total = jnp.sum(K.dwb[k], axis=0, keepdims=True)
        for m in range(4):
            K.hp_sum[0, 40 + 4 * k + m : 41 + 4 * k + m, :] = total[:, 128 * m : 128 * m + 128]
    skip = jnp.zeros((8, 128), F32)
    for g in range(NG):
        skip = skip + mm(jnp.concatenate(split2(K.dD[:, 128 * g : 128 * g + 128]), axis=1), K.R[g, :256, :], 1, 0)
    spread_eye = iota((NH, 128), 0) == iota((NH, 128), 1)

    def as_row(ref):
        total = jnp.sum(ref[...], axis=1, keepdims=True)
        return jnp.sum(jnp.where(spread_eye, jnp.broadcast_to(total, (NH, 128)), 0.0), axis=0, keepdims=True)

    K.hp_sum[0, 56:57, :] = as_row(K.dlr)
    K.hp_sum[0, 57:58, :] = as_row(K.ddr)
    K.hp_sum[0, 58:59, :] = jnp.sum(skip, axis=0, keepdims=True)

    z_at, x_at, y_at = lax.rem(me, 4), lax.rem(me // 4, 2), me // 8
    axes = (
        (4, z_at, lambda k: {"dp": me - z_at + lax.rem(z_at + k, 4)}),
        (4, y_at, lambda k: {"dp": me - 8 * y_at + 8 * lax.rem(y_at + k, 4)}),
        (2, x_at, lambda k: {"dp": me + 4 - 8 * x_at}),
    )

    def exchange(src, hold, size, at, peer, sem):
        return [
            pltpu.make_async_remote_copy(
                src_ref=src, dst_ref=hold.at[at], send_sem=K.gsem.at[sem, 0, k], recv_sem=K.gsem.at[sem, 1, k],
                device_id=peer(k), device_id_type=mesh_ids,
            )
            for k in range(1, size)
        ]

    def param_step(i, start):
        size, at, peer = axes[i]
        if not many:
            if not start:
                K.hp_sum[i + 1] = K.hp_sum[i]
            return
        copies = exchange(K.hp_sum.at[i], K.hp_in.at[i], size, at, peer, i)
        if start:
            for one in copies:
                one.start()
            K.hp_in[i, at] = K.hp_sum[i]
        else:
            for one in copies:
                one.wait()
            total = K.hp_in[i, 0]
            for k in range(1, size):
                total = total + K.hp_in[i, k]
            K.hp_sum[i + 1] = total

    param_step(0, True)

    sums[3].go(1)
    sums[2].go(2)
    re.turn()
    param_step(0, False)
    param_step(1, True)
    sums[3].go(2)

    rd.end()
    for half in range(2):
        lanes = slice(128 * half, 128 * half + 128)
        dv = gather_rows(K.vr, 0, half) * K.gpb[0:T, lanes]
        K.psum[:, lanes] += conv_back(dv, taps(K.cbc, lanes), u=half)
    prompt_sum = TensorSum(K.psum, K.pfull, K.precv, 0, 12)
    prompt_sum.go(0)
    rb.end()

    def prompt_final(k):
        for half in range(2):
            g = 5 * half + k
            lanes = lanes_of(g)
            cum = cum_pair(0, g)
            lu = jnp.exp(cum[T - 1 : T, :] - cum) * gather_rows(K.br, k, half)
            dt = K.dtE[0:T, lanes]
            xlu = K.pxc[:, lanes] * lu
            K.accq[...] += reduce_heads(g, dt * xlu, xlu)
            K.pdxf[:, lanes] += conv_back(dt * lu * K.pgp[:, lanes], taps(K.cw, lanes), u=half)

    param_step(1, False)
    param_step(2, True)
    prompt_sum.go(1)
    pl.loop(0, 5)(prompt_final)
    K.o_pddt[...] += state_steps(K.accq, 0)[1]
    param_step(2, False)
    for j in range(4):
        sums[j].go(3)
    store_rdbc = pltpu.make_async_copy(K.rdbc, K.rdbc_out, K.osem.at[2])
    store_rdbc.start()
    prompt_sum.go(2)
    re.end()
    K.tailx[...] = jnp.zeros((8, CHD), F32)
    K.tailb[...] = jnp.zeros((8, BCW), F32)
    for r, ref, row, lanes in tail_rows(K.tailx, K.tailb):
        ref[row, lanes] = K.er[r // 2, r % 2 : r % 2 + 1, :]
    K.pdxf[120:128, :] += K.tailx[...]
    K.pdx[...] = K.pdxf[...].astype(BF)
    store_pdx = pltpu.make_async_copy(K.pdx, K.pdx_out, K.osem.at[3])
    store_pdx.start()

    K.cb_out[0:16, :] = jnp.zeros((16, 128), F32)
    for i in range(3):
        for m in range(4):
            K.cb_out[4 * i + m : 4 * i + m + 1, :] = K.tailb[5 + i : 6 + i, 128 * m : 128 * m + 128]
    K.cb_out[16:32, :] = K.hp_sum[3, 40:56, :]
    if many:
        last = exchange(K.cb_out, K.cb_in, nt, mt, lambda k: {"tensor": lax.rem(mt + k, nt)}, 3)
        for one in last:
            one.start()
        K.cb_in[mt] = K.cb_out[...]
    for k in range(4):
        for g in range(NG):
            K.o_cw[k : k + 1, 128 * g : 128 * g + 128] = K.hp_sum[3, k * NG + g : k * NG + g + 1, :]
    K.o_hp[...] = K.hp_sum[3, 56:59, 0:NH]
    prompt_sum.go(3)
    K.o_pdbc[...] = K.pfull[...]
    if many:
        for one in last:
            one.wait()
        total = K.cb_in[0]
        for k in range(1, nt):
            total = total + K.cb_in[k]
    else:
        total = K.cb_out[...]
    for m in range(4):
        lanes = slice(128 * m, 128 * m + 128)
        for i in range(3):
            K.o_pdbc[125 + i : 126 + i, lanes] += total[4 * i + m : 4 * i + m + 1, :]
        for k in range(4):
            K.o_cbc[k : k + 1, lanes] = total[16 + 4 * k + m : 17 + 4 * k + m, :]
    for one in (store_rdx, store_out, store_rdbc, store_pdx):
        one.wait()


def finish(*refs):
    count = len(refs) // 3
    sems = refs[-1]
    come = [pltpu.make_async_copy(refs[i], refs[2 * count + i], sems.at[0, i]) for i in range(count)]
    leave = [pltpu.make_async_copy(refs[2 * count + i], refs[count + i], sems.at[1, i]) for i in range(count)]
    for one in come:
        one.start()
    for one, two in zip(come, leave):
        one.wait()
        two.start()
    for one in leave:
        one.wait()


def body(n, nt, *args):
    (px, pbc, pdt, pz, rx, rbc, rdt, rz, cw, cbc, hp, of, rlen, pcot, rcot) = args
    given = dict(px=px, pbc=pbc, pdt=pdt, pz=pz, pcot=pcot, rx=rx, rbc=rbc, rdt=rdt, rz=rz, rcot=rcot, cw=cw, cbc=cbc, hp=hp)
    vm = pl.BlockSpec(memory_space=pltpu.VMEM)
    sm = pl.BlockSpec(memory_space=pltpu.SMEM)
    far = pl.BlockSpec(memory_space=pl.ANY)
    shape = jax.ShapeDtypeStruct
    small = dict(
        o_pdbc=(T, BCW), o_pddt=(NH, T), o_rddt=(NH, 512), o_cw=(4, CHD), o_cbc=(4, BCW), o_hp=(3, NH)
    )
    params = dict(vmem_limit_bytes=62 * 1024 * 1024, has_side_effects=True)
    if n > 1:
        params["collective_id"] = 0
    shapes = [shape(*SHAPES[name]) for name in BIG_OUT] + [shape(small[name], F32) for name in SMALL_OUT]
    results = pl.pallas_call(
        functools.partial(kernel, n, nt),
        out_shape=tuple(shapes),
        in_specs=[far] * len(BIG_IN) + [vm] * len(SMALL_IN) + [sm] * len(SCALARS),
        out_specs=tuple([far] * len(BIG_OUT) + [vm] * len(SMALL_OUT)),
        scratch_shapes=list(scratch_table().values()),
        compiler_params=pltpu.CompilerParams(**params),
    )(*[given[name] for name in BIG_IN + SMALL_IN], of, rlen)
    results = pl.pallas_call(
        finish,
        out_shape=tuple(shapes),
        in_specs=[far] * len(shapes),
        out_specs=tuple([far] * len(shapes)),
        scratch_shapes=[pltpu.VMEM(one.shape, one.dtype) for one in shapes] + [pltpu.SemaphoreType.DMA((2, len(shapes)))],
        compiler_params=pltpu.CompilerParams(vmem_limit_bytes=62 * 1024 * 1024),
    )(*results)
    got = dict(zip(BIG_OUT + SMALL_OUT, results))
    order = ("out", "pdx", "o_pdbc", "o_pddt", "rdx", "rdbc", "o_rddt", "o_cw", "o_cbc", "o_hp")
    return tuple(got[name] for name in order)


def solution(mesh):
    n = mesh.shape["dp"]
    nt = mesh.shape["tensor"]
    placed = (
        P("dp", "tensor"), P("dp", None), P("tensor", "dp"), P("dp", "tensor"),
        P("dp", "tensor"), P("dp", None), P("tensor", "dp"), P("dp", "tensor"),
        P(None, "tensor"), P(), P(None, "tensor"), P(), P("dp", None),
        P("dp", "tensor"), P("dp", "tensor"),
    )
    return jax.shard_map(
        functools.partial(body, n, nt),
        mesh=mesh,
        in_specs=placed,
        out_specs=(
            P("dp", "tensor"), P("dp", "tensor"), P("dp", None), P("tensor", "dp"),
            P("dp", "tensor"), P("dp", None), P("tensor", "dp"),
            P(None, "tensor"), P(), P(None, "tensor"),
        ),
        check_vma=False,
    )
```

```python
import functools
import types

import jax
import jax.numpy as jnp
from jax import lax
from jax.experimental import pallas as pl
from jax.experimental.pallas import tpu as pltpu
from jax.sharding import PartitionSpec as P

F32 = jnp.float32
BF = jnp.bfloat16
T = 128
NH = 20
NG = 10
NS = 256
CHD = 1280
BCW = 512
UNROLL = 5
ROW = 40
SMALL = 10


def mm(a, b, ca, cb):
    return lax.dot_general(a, b, (((ca,), (cb,)), ((), ())), preferred_element_type=F32)


def split2(a):
    hi = a.astype(BF)
    return hi, (a - hi.astype(F32)).astype(BF)


def split3(a):
    hi = a.astype(BF)
    rest = a - hi.astype(F32)
    mid = rest.astype(BF)
    return hi, mid, (rest - mid.astype(F32)).astype(BF)


def mm3(a, b, ca, cb):
    ah, al = split2(a)
    bh, bl = split2(b)
    return mm(ah, bh, ca, cb) + mm(ah, bl, ca, cb) + mm(al, bh, ca, cb)


def mmx(a, ones, ca, cb):
    hi, mid, lo = split3(a)
    return mm(hi, ones, ca, cb) + mm(mid, ones, ca, cb) + mm(lo, ones, ca, cb)


def sigmoid(v):
    return 0.5 + 0.5 * jnp.tanh(0.5 * v)


def softplus(u):
    e = jnp.exp(-jnp.abs(u))
    s = e / (2.0 + e)
    q = s * s
    poly = 1.0 + q * (1 / 3 + q * (1 / 5 + q * (1 / 7 + q * (1 / 9 + q * (1 / 11 + q / 13)))))
    return jnp.maximum(u, 0.0) + 2.0 * s * poly


def iota(shape, dim):
    return lax.broadcasted_iota(jnp.int32, shape, dim)


def fold8(a):
    return jnp.sum(a.reshape(16, 8, 128), axis=0)


BIG_IN = ("px", "pbc", "pdt", "cw", "cbc", "hp", "rdt", "pz", "pcot", "rz", "rcot", "rx", "rbc")
SCALARS = ("of", "rlen")
BIG_OUT = ("out", "pdx", "rdx", "rdbc", "o_pdbc", "o_pddt", "o_rddt", "o_cw", "o_cbc", "o_hp")
SHAPES = dict(
    px=((T, CHD), BF), pbc=((T, BCW), BF), pz=((T, CHD), BF), pcot=((T, CHD), BF),
    rx=((512, CHD), BF), rbc=((512, BCW), BF), rz=((512, CHD), BF), rcot=((512, CHD), BF),
    pdt=((NH, T), F32), rdt=((NH, 512), F32), cw=((4, CHD), F32), cbc=((4, BCW), F32), hp=((3, NH), F32),
    o_pdbc=((T, BCW), F32), o_pddt=((NH, T), F32), o_rddt=((NH, 512), F32), o_cw=((4, CHD), F32),
    o_cbc=((4, BCW), F32), o_hp=((3, NH), F32),
    out=((512, CHD), BF), pdx=((T, CHD), BF), rdx=((512, CHD), BF), rdbc=((512, BCW), F32),
)


def scratch_table():
    v = pltpu.VMEM
    dma = pltpu.SemaphoreType.DMA
    table = {name: v(*SHAPES[name]) for name in BIG_IN + BIG_OUT}
    for one in "tfbv":
        rows = {"t": SMALL, "f": ROW, "b": ROW, "v": SMALL}[one]
        for part in "shlr":
            table[one + part] = v((32, rows, 128), F32)
    table.update(
        hp_sum=v((4, 64, 128), F32), par_in=v((3, 4, 64, 128), F32), cb_in=v((4, 32, 128), F32), cb_out=v((32, 128), F32),
        rsum=v((512, BCW), F32), rrecv=v((4, 2, 64, BCW), F32),
        psum=v((T, BCW), F32), pfull=v((T, BCW), F32), precv=v((2, 64, BCW), F32),
        invv=v((1, 128), jnp.int32), inv=pltpu.SMEM((1, 128), jnp.int32),
        adt=v((NH, T), F32),
        dtr=v((6, NH, T), F32), sig=v((6, NH, T), F32), lr=v((6, NH, T), F32), cumr=v((6, NH, T), F32),
        tmp=v((6, 128, 128), F32), col=v((2, NH, 1), F32), dex=v((1, CHD), F32),
        cumB=v((6 * NH, T, T), F32), dtE=v((6 * T, CHD), F32),
        R=v((NG, 512, 128), BF), Gcol=v((12, T, T), F32), dGcol=v((12, T, T), F32),
        B=v((6, T, NS), F32), C=v((5, T, NS), F32), Cb=v((5, T, NS), BF), gpb=v((6 * T, BCW), F32),
        G=v((5, T, T), F32), dG=v((5, T, T), F32), acc=v((6, T, 128), F32), accq=v((T, 128), F32),
        xs=v((5, 136, 128), F32), ds=v((5, 144, 128), F32),
        tailx=v((8, CHD), F32), tailb=v((8, BCW), F32), dtailx=v((8, CHD), F32), dtailb=v((8, BCW), F32),
        dw=v((4, 8, CHD), F32), dwb=v((4, 8, BCW), F32), dD=v((8, CHD), F32),
        pxc=v((T, CHD), F32), pgp=v((T, CHD), F32), pdxf=v((T, CHD), F32),
        live=v((512, 128), F32), dy=v((512, CHD), F32), sz=v((512, CHD), F32),
        edy=v((512, CHD), BF), ee=v((512, CHD), F32),
        S=v((CHD, NS), BF), dS=v((CHD, NS), BF),
        dlr=v((NH, T), F32), ddr=v((NH, T), F32),
        sem=dma((8, 2, 32)), tsem=dma((16, 2)), gsem=dma((4, 2, 4)), isem=dma((len(BIG_IN) + 1,)), osem=dma((len(BIG_OUT),)),
    )
    return table


def kernel(n, nt, *refs):
    names = [name + "_in" for name in BIG_IN] + list(SCALARS)
    names += [name + "_out" for name in BIG_OUT] + list(scratch_table())
    K = types.SimpleNamespace(**dict(zip(names, refs)))
    me = lax.axis_index("dp")
    mt = lax.axis_index("tensor")
    left = iota((T, 128), 1) < 64
    lower = iota((T, T), 0) >= iota((T, T), 1)
    mesh_ids = pl.DeviceIdType.MESH
    many = n > 1

    if many:
        barrier = pltpu.get_barrier_semaphore()

        def greet(k):
            pl.semaphore_signal(barrier, inc=1, device_id={"dp": lax.rem(me + k, n)}, device_id_type=mesh_ids)

        pl.loop(1, n)(greet)
        for k in range(1, nt):
            pl.semaphore_signal(barrier, inc=1, device_id={"tensor": lax.rem(mt + k, nt)}, device_id_type=mesh_ids)

    loads = {
        name: pltpu.make_async_copy(getattr(K, name + "_in"), getattr(K, name), K.isem.at[i])
        for i, name in enumerate(BIG_IN)
    }
    for name in BIG_IN:
        loads[name].start()

    class Relay:
        def __init__(self, key, sem, table):
            self.s, self.h, self.l, self.r = (getattr(K, key + part) for part in "shlr")
            self.sem = sem
            self.table = table

        def copy(self, src, dst, sem):
            def one(k):
                peer = lax.rem(me + k, n)
                return pltpu.make_async_remote_copy(
                    src_ref=src.at[peer], dst_ref=dst.at[me], send_sem=K.sem.at[sem, 0, k], recv_sem=K.sem.at[sem, 1, k],
                    device_id={"dp": peer}, device_id_type=mesh_ids,
                )

            return one

        def send(self):
            if many:
                one = self.copy(self.s, self.h, self.sem)
                pl.loop(1, n)(lambda k: one(k).start())
                self.h[me] = self.s[me]

        def turn(self):
            if many:
                one = self.copy(self.s, self.h, self.sem)
                pl.loop(1, n)(lambda k: one(k).wait())

                def pick(d):
                    self.l[d] = self.h[self.table(d)]

                pl.loop(0, n)(pick)
                two = self.copy(self.l, self.r, self.sem + 1)
                pl.loop(1, n)(lambda k: two(k).start())
                self.r[me] = self.l[me]

        def end(self):
            if many:
                two = self.copy(self.l, self.r, self.sem + 1)
                pl.loop(1, n)(lambda k: two(k).wait())
            else:
                self.r[...] = self.s[...]

    forth = lambda d: K.of[d]
    home = lambda d: K.inv[0, d]
    rt, rf = Relay("t", 0, forth), Relay("f", 2, forth)
    rb, rd = Relay("b", 4, home), Relay("v", 6, home)

    def lanes_of(g):
        return pl.ds(pl.multiple_of(g * 128, 128), 128)

    def rows_of(q):
        return pl.ds(pl.multiple_of(q * T, T), T)

    def scatter_rows(ref, k, half, tile):
        spot = pl.ds(pl.multiple_of(8 * k, 8), 8)
        for i in range(16):
            ref[2 * i + half, spot, :] = tile[8 * i : 8 * i + 8, :]

    def gather_rows(ref, k, half):
        spot = pl.ds(pl.multiple_of(8 * k, 8), 8)
        return jnp.concatenate([ref[2 * i + half, spot, :] for i in range(16)], axis=0)

    def tail_rows(rows_x, rows_b):
        for r in range(42):
            i, m = divmod(r, 14)
            ref, m = (rows_x, m) if m < 10 else (rows_b, m - 10)
            yield r, ref, slice(5 + i, 6 + i), slice(128 * m, 128 * m + 128)

    for name in BIG_IN[:7]:
        loads[name].wait()
    K.tailx[...] = K.px[112:128, :].astype(F32)[8:16, :]
    K.tailb[...] = K.pbc[112:128, :].astype(F32)[8:16, :]
    K.ts[:, 8:10, :] = jnp.zeros((32, 2, 128), F32)
    for r, ref, row, lanes in tail_rows(K.tailx, K.tailb):
        K.ts[r // 2, 8 + r % 2 : 9 + r % 2, :] = ref[row, lanes]
    for h in range(NH):
        r = 42 + h
        K.ts[r // 2, 8 + r % 2 : 9 + r % 2, :] = K.pdt[h : h + 1, :]
    for half in range(2):
        scatter_rows(K.ts, 0, half, K.pbc[:, 128 * half : 128 * half + 128].astype(F32))

    def pack_x(k):
        for half in range(2):
            scatter_rows(K.fs, k, half, K.px[:, lanes_of(5 * half + k)].astype(F32))

    if many:
        pl.semaphore_wait(barrier, n - 1 + nt - 1)
    rt.send()
    pl.loop(0, 5)(pack_x)
    rf.send()

    tri = (iota((T, T), 0) <= iota((T, T), 1)).astype(F32).astype(BF)
    trir = (iota((T, T), 0) >= iota((T, T), 1)).astype(F32).astype(BF)
    tris = (iota((T, T), 0) < iota((T, T), 1)).astype(F32).astype(BF)
    eye = iota((NH, NH), 0) == iota((NH, NH), 1)

    lane = iota((1, 128), 1)
    back_to = jnp.zeros((1, 128), jnp.int32)
    for d in range(n):
        back_to = jnp.where(lane == K.of[d], d, back_to)
    K.invv[...] = back_to
    inv_copy = pltpu.make_async_copy(K.invv, K.inv, K.isem.at[len(BIG_IN)])
    inv_copy.start()

    def column(row):
        return jnp.sum(jnp.where(eye, jnp.broadcast_to(K.hp[row : row + 1, :], (NH, NH)), 0.0), axis=1, keepdims=True)

    K.col[0] = -jnp.exp(column(0))
    K.col[1] = column(1)
    for g in range(NG):
        K.dex[:, 128 * g : 128 * g + 128] = jnp.where(
            lane < 64, K.hp[2:3, 2 * g : 2 * g + 1], K.hp[2:3, 2 * g + 1 : 2 * g + 2]
        )
    for j in range(4):
        K.live[j * T : j * T + T, :] = jnp.where(iota((T, 128), 0) < K.rlen[0, j], 1.0, 0.0)

    def make_R(g):
        r = iota((512, 128), 0)
        want = 2 * g + jnp.where((r & 127) >= 64, 1, 0) + jnp.where(r >= 256, 32, 0)
        K.R[g] = (iota((512, 128), 1) == want).astype(F32).astype(BF)

    pl.loop(0, NG)(make_R)
    for name in ("dG", "acc", "accq", "dw", "dwb", "dD", "dtailx", "dtailb", "dGcol", "dlr", "ddr", "ds", "tmp"):
        ref = getattr(K, name)
        ref[...] = jnp.zeros(ref.shape, F32)

    def step_tables(dt_ref, ats, qs):
        every = list(zip(ats, qs))
        for at, q in every:
            u = dt_ref[:, at * T : at * T + T] + K.col[1]
            dt = softplus(u)
            lr = K.col[0] * dt
            cum = mmx(lr, tri, 1, 0)
            K.sig[q] = 1.0 / (1.0 + jnp.exp(-u))
            K.lr[q] = lr
            K.cumr[q] = cum
            K.tmp[q, 0:NH, :] = cum
            K.tmp[q, 32 : 32 + NH, :] = dt
        for at, q in every:
            cols = K.tmp[q].T
            for h in range(NH):
                K.cumB[q * NH + h] = jnp.broadcast_to(cols[:, h : h + 1], (T, T))
            for g in range(NG):
                a = 32 + 2 * g
                K.dtE[q * T : q * T + T, 128 * g : 128 * g + 128] = jnp.where(
                    left, jnp.broadcast_to(cols[:, a : a + 1], (T, 128)), jnp.broadcast_to(cols[:, a + 1 : a + 2], (T, 128))
                )

    def conv(x, tail, w, u=0):
        K.xs[u, 0:8, :] = tail
        K.xs[u, 8:136, :] = x
        v = w[0] * K.xs[u, 5:133, :] + w[1] * K.xs[u, 6:134, :] + w[2] * K.xs[u, 7:135, :] + w[3] * x
        s = sigmoid(v)
        xc = v * s
        return xc, s + xc * (1.0 - s)

    def conv_taps(dv, dw_ref, lanes, u=0):
        for k in range(4):
            dw_ref[k, :, lanes] += fold8(dv * K.xs[u, 5 + k : 133 + k, :])

    def tail_back(dv, w, tail_ref, lanes, u):
        K.ds[u, 8:16, :] = dv
        tail_ref[:, lanes] += w[0] * K.ds[u, 3:11, :] + w[1] * K.ds[u, 2:10, :] + w[2] * K.ds[u, 1:9, :]

    def conv_back(dv, w, u=0):
        K.ds[u, 8:136, :] = dv
        return w[3] * dv + w[2] * K.ds[u, 9:137, :] + w[1] * K.ds[u, 10:138, :] + w[0] * K.ds[u, 11:139, :]

    def taps(ref, lanes):
        return [ref[k : k + 1, lanes] for k in range(4)]

    no_tail = jnp.zeros((8, 128), F32)

    def bc_forward(bc_ref, at, q, tail, u=0):
        for m in range(4):
            lanes = slice(128 * m, 128 * m + 128)
            xc, gp = conv(bc_ref[rows_of(at), lanes].astype(F32), tail(lanes), taps(K.cbc, lanes), m)
            K.gpb[rows_of(q), lanes] = gp
            if m < 2:
                K.B[q, :, lanes] = xc
            else:
                half = slice(128 * (m - 2), 128 * (m - 2) + 128)
                K.C[q, :, half] = xc
                K.Cb[q, :, half] = xc.astype(BF)
        K.G[q] = jnp.where(lower, mm3(K.C[q], K.B[q], 1, 1), 0.0)

    def bc_back(bc_ref, at, q, tail, dc_more, o_ref):
        dgm = jnp.where(lower, K.dG[q], 0.0)
        dc = mm3(dgm, K.B[q], 1, 0) + dc_more
        db = mm3(dgm, K.C[q], 0, 0)
        for m in range(4):
            lanes = slice(128 * m, 128 * m + 128)
            d = db[:, lanes] if m < 2 else dc[:, 128 * (m - 2) : 128 * (m - 2) + 128]
            dv = d * K.gpb[rows_of(q), lanes]
            K.xs[m, 0:8, :] = tail(lanes)
            K.xs[m, 8:136, :] = bc_ref[rows_of(at), lanes].astype(F32)
            conv_taps(dv, K.dwb, lanes, m)
            o_ref[rows_of(at), lanes] = conv_back(dv, taps(K.cbc, lanes), m)

    def cum_pair(q, g):
        return jnp.where(left, K.cumB[q * NH + 2 * g], K.cumB[q * NH + 2 * g + 1])

    def attend(q, g, xc, dy, dt):
        xd = dt * xc
        x2 = jnp.concatenate([jnp.where(left, xd, 0.0).astype(BF), jnp.where(left, 0.0, xd).astype(BF)], axis=0)
        d2 = jnp.concatenate([jnp.where(left, dy, 0.0).astype(BF), jnp.where(left, 0.0, dy).astype(BF)], axis=0)
        xdb = xd.astype(BF)
        dyb = dy.astype(BF)
        scores = K.G[q]
        decay = [
            jnp.exp(jnp.minimum(K.cumB[q * NH + 2 * g + i] - K.cumr[q, pl.ds(2 * g + i, 1), :], 0.0)) for i in range(2)
        ]
        mix = [(scores * one).astype(BF) for one in decay]
        yin = mm(jnp.concatenate(mix, axis=1), x2, 1, 0)
        dxd = mm(jnp.concatenate(mix, axis=0), d2, 0, 0)
        dmix = mm(dyb, x2, 1, 1)
        K.dG[q] += dmix[:, :T] * decay[0] + dmix[:, T:] * decay[1]
        return yin, dxd, xdb.astype(F32), dyb.astype(F32)

    def reduce_heads(g, first, second=None):
        parts = list(split2(first))
        if second is not None:
            parts += split2(second)
        return mm(jnp.concatenate(parts, axis=1), K.R[g, : 128 * len(parts), :], 1, 0)

    def steps_back(q, o_ref, at):
        a = K.acc[q].T
        dlr = mmx(a[0:NH, :], trir, 1, 0)
        draw = (a[32 : 32 + NH, :] + K.col[0] * dlr) * K.sig[q]
        o_ref[:, pl.ds(pl.multiple_of(at * T, T), T)] = draw
        K.dlr[...] += K.lr[q] * dlr
        K.ddr[...] += draw

    def state_steps(acc, q):
        a = acc[...].T
        dlr = mmx(a[0:NH, :], tris, 1, 0)
        return dlr, (a[32 : 32 + NH, :] + K.col[0] * dlr) * K.sig[q]

    step_tables(K.pdt, [0], [0])
    bc_forward(K.pbc, 0, 0, lambda lanes: no_tail)
    loads["pz"].wait()
    loads["pcot"].wait()

    def prompt_local(i):
        for u in range(UNROLL):
            g = i * UNROLL + u
            lanes = lanes_of(g)
            w = taps(K.cw, lanes)
            xc, gp = conv(K.px[:, lanes].astype(F32), no_tail, w, u)
            K.pxc[:, lanes] = xc
            K.pgp[:, lanes] = gp
            z = K.pz[:, lanes].astype(F32)
            dy = K.pcot[:, lanes].astype(F32) * (z * sigmoid(z))
            dt = K.dtE[0:T, lanes]
            yin, dxd, xdr, dyr = attend(0, g, xc, dy, dt)
            K.acc[0] += reduce_heads(g, dyr * yin - xdr * dxd, xc * dxd)
            K.dD[:, lanes] += fold8(dy * xc)
            dv = (dt * dxd + K.dex[:, lanes] * dy) * gp
            conv_taps(dv, K.dw, lanes, u)
            K.pdxf[:, lanes] = conv_back(dv, w, u)

    pl.loop(0, NG // UNROLL)(prompt_local)
    bc_back(K.pbc, 0, 0, lambda lanes: no_tail, 0.0, K.psum)
    steps_back(0, K.o_pddt, 0)

    rt.turn()

    step_tables(K.rdt, [0, 1, 2, 3], [1, 2, 3, 4])
    loads["rz"].wait()
    loads["rcot"].wait()

    def gates(i):
        j = i // NG
        g = lax.rem(i, NG)
        lanes = lanes_of(g)
        rows = rows_of(j)
        z = K.rz[rows, lanes].astype(F32)
        sz = z * sigmoid(z)
        dy = K.rcot[rows, lanes].astype(F32) * (sz * K.live[rows, :])
        e = jnp.exp(cum_pair(j + 1, g))
        K.sz[rows, lanes] = sz
        K.dy[rows, lanes] = dy
        K.ee[rows, lanes] = e
        K.edy[rows, lanes] = (e * dy).astype(BF)

    pl.loop(0, 4 * NG, unroll=2)(gates)
    rf.turn()
    loads["rx"].wait()
    loads["rbc"].wait()
    inv_copy.wait()
    rt.end()

    for r, ref, row, lanes in tail_rows(K.tailx, K.tailb):
        ref[row, lanes] = K.tr[r // 2, 8 + r % 2 : 9 + r % 2, :]
    for h in range(NH):
        r = 42 + h
        K.adt[h : h + 1, :] = K.tr[r // 2, 8 + r % 2 : 9 + r % 2, :]
    for j in range(4):
        bc_forward(K.rbc, j, j + 1, lambda lanes: K.tailb[:, lanes])
    for half in range(2):
        lanes = slice(128 * half, 128 * half + 128)
        xc, gp = conv(gather_rows(K.tr, 0, half), no_tail, taps(K.cbc, lanes), half)
        K.B[5, :, lanes] = xc
        K.gpb[5 * T : 6 * T, lanes] = gp

    def state_grad(k):
        bh = K.B[5].astype(BF)
        for half in range(2):
            lanes = lanes_of(5 * half + k)
            ds = mm(K.edy[:, lanes], K.Cb[1:5].reshape(4 * T, NS), 0, 0).astype(BF)
            K.dS[lanes, :] = ds
            scatter_rows(K.bs, k, half, mm(bh, ds, 1, 1))

    pl.loop(0, 5)(state_grad)
    rb.send()
    step_tables(K.adt, [0], [5])

    row8 = iota((8, 128), 0)
    for j in range(4):
        for t in range(3):
            K.Gcol[3 * j + t] = jnp.broadcast_to(K.G[j + 1, :, t : t + 1], (T, T))

    def first_rows(j):
        def five(i):
            for u in range(UNROLL):
                g = i * UNROLL + u
                lanes = lanes_of(g)
                w = taps(K.cw, lanes)
                K.xs[u, 0:8, :] = K.tailx[:, lanes]
                K.xs[u, 8:24, :] = K.rx[pl.ds(j * T, 16), lanes].astype(F32)
                v = (w[0] * K.xs[u, 5:13, :] + w[1] * K.xs[u, 6:14, :] + w[2] * K.xs[u, 7:15, :]
                     + w[3] * K.xs[u, 8:16, :])
                sg = sigmoid(v)
                xc = v * sg
                gp = sg + xc * (1.0 - sg)
                dt = K.dtE[pl.ds((j + 1) * T, 8), lanes]
                xd = dt * xc
                dy = K.dy[rows_of(j), lanes]
                cum = cum_pair(j + 1, g)
                dxd = jnp.zeros((8, 128), F32)
                for t in range(3):
                    m = jnp.exp(jnp.minimum(cum - cum[t : t + 1, :], 0.0)) * dy
                    K.dGcol[3 * j + t] += m * xd[t : t + 1, :]
                    dxd = jnp.where(row8 == t, jnp.sum(K.Gcol[3 * j + t] * m, axis=0, keepdims=True), dxd)
                dv = (dt * dxd + K.dex[:, lanes] * dy[0:8, :]) * gp
                tail_back(jnp.where(row8 < 3, dv, 0.0), w, K.dtailx, lanes, u)

        pl.loop(0, NG // UNROLL)(five)

    def first_bc_rows(j):
        more = mm(K.edy[pl.ds(j * T, 16), :], K.S[...], 1, 0)[0:8, :]
        r8 = iota((8, NS), 0)
        dc = more
        db = jnp.zeros((8, NS), F32)
        for t in range(3):
            col = jnp.sum(K.dGcol[3 * j + t], axis=1, keepdims=True)
            col = jnp.where(iota((T, 1), 0) >= t, col, 0.0)
            dc = dc + col[0:8, :] * K.B[j + 1, t : t + 1, :]
            db = jnp.where(r8 == t, jnp.sum(col * K.C[j + 1], axis=0, keepdims=True), db)
        for m in range(4):
            lanes = slice(128 * m, 128 * m + 128)
            d = db[:, lanes] if m < 2 else dc[:, 128 * (m - 2) : 128 * (m - 2) + 128]
            dv = jnp.where(row8 < 3, d * K.gpb[pl.ds((j + 1) * T, 8), lanes], 0.0)
            tail_back(dv, taps(K.cbc, lanes), K.dtailb, lanes, m)

    for j in range(4):
        first_rows(j)

    def resp_local(j):
        def five(i):
            for u in range(UNROLL):
                g = i * UNROLL + u
                lanes = lanes_of(g)
                rows = rows_of(j)
                w = taps(K.cw, lanes)
                xc, gp = conv(K.rx[rows, lanes].astype(F32), K.tailx[:, lanes], w, u)
                dy = K.dy[rows, lanes]
                dt = K.dtE[rows_of(j + 1), lanes]
                yin, dxd, xdr, dyr = attend(j + 1, g, xc, dy, dt)
                gain = K.dex[:, lanes]
                y = yin + gain * xc
                steps = dyr * yin - xdr * dxd
                cs = mm(K.Cb[j + 1], K.S[lanes, :], 1, 1)
                K.out[rows, lanes] = ((y + K.ee[rows, lanes] * cs) * K.sz[rows, lanes]).astype(BF)
                steps = steps + K.edy[rows, lanes].astype(F32) * cs
                K.acc[j + 1] += reduce_heads(g, steps, xc * dxd)
                K.dD[:, lanes] += fold8(dy * xc)
                dv = (dt * dxd + gain * dy) * gp
                conv_taps(dv, K.dw, lanes, u)
                K.rdx[rows, lanes] = conv_back(dv, w, u).astype(BF)

        pl.loop(0, NG // UNROLL)(five)

    def resp_bc_back(j):
        more = mm(K.edy[rows_of(j), :], K.S[...], 1, 0)
        bc_back(K.rbc, j, j + 1, lambda lanes: K.tailb[:, lanes], more, K.rsum)

    core = lax.rem(mt, 2)
    mate = mt + 1 - 2 * core
    across = lax.rem(mt + 2, 4)

    class TensorSum:
        def __init__(self, buf, full, recv, base, at):
            mine = pl.ds(pl.multiple_of(base + core * 64, 8), 64)
            other = pl.ds(pl.multiple_of(base + (1 - core) * 64, 8), 64)
            self.buf, self.full, self.recv, self.base, self.mine = buf, full, recv, base, mine
            plan = ((buf.at[other, :], recv.at[0], mate), (buf.at[mine, :], recv.at[1], across),
                    (buf.at[mine, :], full.at[mine, :], mate))
            self.steps = [
                pltpu.make_async_remote_copy(
                    src_ref=src, dst_ref=dst, send_sem=K.tsem.at[at + i, 0], recv_sem=K.tsem.at[at + i, 1],
                    device_id={"tensor": peer}, device_id_type=mesh_ids,
                )
                for i, (src, dst, peer) in enumerate(plan)
            ] if many else None

        def go(self, stage):
            if not many:
                if stage == 0:
                    rows = pl.ds(self.base, T)
                    self.full[rows, :] = self.buf[rows, :]
                return
            if stage > 0:
                self.steps[stage - 1].wait()
            if stage in (1, 2):
                self.buf[self.mine, :] += self.recv[stage - 1]
            if stage == 2:
                self.full[self.mine, :] = self.buf[self.mine, :]
            if stage < 3:
                self.steps[stage].start()

    sums = [TensorSum(K.rsum, K.rdbc, K.rrecv.at[j], j * T, 3 * j) for j in range(4)]

    rf.end()

    def adopt(k, dbp):
        bh, bl = split2(K.B[5])
        for half in range(2):
            g = 5 * half + k
            lanes = lanes_of(g)
            xc, gp = conv(gather_rows(K.fr, k, half), no_tail, taps(K.cw, lanes), half)
            cum = cum_pair(5, g)
            lv = jnp.exp(cum[T - 1 : T, :] - cum)
            dt = K.dtE[5 * T : 6 * T, lanes]
            xd = dt * xc
            xh, xl = split2(lv * xd)
            K.S[lanes, :] = (mm(xh, bh, 0, 0) + mm(xh, bl, 0, 0) + mm(xl, bh, 0, 0)).astype(BF)
            dbp = dbp + mm(xh, K.dS[lanes, :], 1, 0)
            lu = lv * gather_rows(K.bs, k, half)
            K.acc[5] += reduce_heads(g, xd * lu, xc * lu)
            conv_taps(dt * lu * gp, K.dw, lanes, half)
        return dbp

    dbp = lax.fori_loop(0, 5, adopt, jnp.zeros((T, NS), F32))
    for half in range(2):
        lanes = slice(128 * half, 128 * half + 128)
        scatter_rows(K.vs, 0, half, dbp[:, lanes])
        K.xs[half, 0:8, :] = no_tail
        K.xs[half, 8:136, :] = gather_rows(K.tr, 0, half)
        conv_taps(dbp[:, lanes] * K.gpb[5 * T : 6 * T, lanes], K.dwb, lanes, half)
    for j in range(4):
        first_bc_rows(j)
    K.vs[:, 8:10, :] = jnp.zeros((32, 2, 128), F32)
    for r, ref, row, lanes in tail_rows(K.dtailx, K.dtailb):
        K.vs[r // 2, 8 + r % 2 : 9 + r % 2, :] = ref[row, lanes]
    rd.send()
    dlr, draw = state_steps(K.acc.at[5], 5)
    K.dlr[...] += K.lr[5] * dlr
    K.ddr[...] += draw

    resp_local(0)
    resp_bc_back(0)
    sums[0].go(0)
    rb.turn()
    resp_local(1)
    resp_bc_back(1)
    sums[0].go(1)
    sums[1].go(0)
    rd.turn()
    resp_local(2)
    resp_bc_back(2)
    sums[0].go(2)
    sums[1].go(1)
    sums[2].go(0)
    resp_local(3)
    resp_bc_back(3)
    sums[3].go(0)
    sums[1].go(2)
    sums[2].go(1)
    store_rdx = pltpu.make_async_copy(K.rdx, K.rdx_out, K.osem.at[0])
    store_rdx.start()
    store_out = pltpu.make_async_copy(K.out, K.out_out, K.osem.at[1])
    store_out.start()

    for j in range(4):
        steps_back(j + 1, K.o_rddt, j)
    K.hp_sum[0] = jnp.zeros((64, 128), F32)
    for k in range(4):
        total = jnp.sum(K.dw[k], axis=0, keepdims=True)
        for g in range(NG):
            K.hp_sum[0, k * NG + g : k * NG + g + 1, :] = total[:, 128 * g : 128 * g + 128]
        total = jnp.sum(K.dwb[k], axis=0, keepdims=True)
        for m in range(4):
            K.hp_sum[0, 40 + 4 * k + m : 41 + 4 * k + m, :] = total[:, 128 * m : 128 * m + 128]
    skip = jnp.zeros((8, 128), F32)
    for g in range(NG):
        skip = skip + mm(jnp.concatenate(split2(K.dD[:, 128 * g : 128 * g + 128]), axis=1), K.R[g, :256, :], 1, 0)
    spread_eye = iota((NH, 128), 0) == iota((NH, 128), 1)

    def as_row(ref):
        total = jnp.sum(ref[...], axis=1, keepdims=True)
        return jnp.sum(jnp.where(spread_eye, jnp.broadcast_to(total, (NH, 128)), 0.0), axis=0, keepdims=True)

    K.hp_sum[0, 56:57, :] = as_row(K.dlr)
    K.hp_sum[0, 57:58, :] = as_row(K.ddr)
    K.hp_sum[0, 58:59, :] = jnp.sum(skip, axis=0, keepdims=True)

    z_at, x_at, y_at = lax.rem(me, 4), lax.rem(me // 4, 2), me // 8
    axes = (
        (4, z_at, lambda k: {"dp": me - z_at + lax.rem(z_at + k, 4)}),
        (4, y_at, lambda k: {"dp": me - 8 * y_at + 8 * lax.rem(y_at + k, 4)}),
        (2, x_at, lambda k: {"dp": me + 4 - 8 * x_at}),
    )

    def exchange(src, hold, size, at, peer, sem):
        return [
            pltpu.make_async_remote_copy(
                src_ref=src, dst_ref=hold.at[at], send_sem=K.gsem.at[sem, 0, k], recv_sem=K.gsem.at[sem, 1, k],
                device_id=peer(k), device_id_type=mesh_ids,
            )
            for k in range(1, size)
        ]

    def param_step(i, start):
        size, at, peer = axes[i]
        if not many:
            if not start:
                K.hp_sum[i + 1] = K.hp_sum[i]
            return
        copies = exchange(K.hp_sum.at[i], K.par_in.at[i], size, at, peer, i)
        if start:
            for one in copies:
                one.start()
            K.par_in[i, at] = K.hp_sum[i]
        else:
            for one in copies:
                one.wait()
            total = K.par_in[i, 0]
            for k in range(1, size):
                total = total + K.par_in[i, k]
            K.hp_sum[i + 1] = total

    param_step(0, True)
    rd.end()
    for half in range(2):
        lanes = slice(128 * half, 128 * half + 128)
        dv = gather_rows(K.vr, 0, half) * K.gpb[0:T, lanes]
        K.psum[:, lanes] += conv_back(dv, taps(K.cbc, lanes), u=half)
    prompt_sum = TensorSum(K.psum, K.pfull, K.precv, 0, 12)
    prompt_sum.go(0)
    sums[3].go(1)
    sums[2].go(2)
    param_step(0, False)
    param_step(1, True)

    def prompt_final(k):
        for half in range(2):
            g = 5 * half + k
            lanes = lanes_of(g)
            cum = cum_pair(0, g)
            lu = jnp.exp(cum[T - 1 : T, :] - cum) * gather_rows(K.br, k, half)
            dt = K.dtE[0:T, lanes]
            xlu = K.pxc[:, lanes] * lu
            K.accq[...] += reduce_heads(g, dt * xlu, xlu)
            K.pdxf[:, lanes] += conv_back(dt * lu * K.pgp[:, lanes], taps(K.cw, lanes), u=half)

    rb.end()
    pl.loop(0, 5)(prompt_final)
    K.tailx[...] = jnp.zeros((8, CHD), F32)
    K.tailb[...] = jnp.zeros((8, BCW), F32)
    for r, ref, row, lanes in tail_rows(K.tailx, K.tailb):
        ref[row, lanes] = K.vr[r // 2, 8 + r % 2 : 9 + r % 2, :]
    K.pdxf[120:128, :] += K.tailx[...]
    K.pdx[...] = K.pdxf[...].astype(BF)
    store_pdx = pltpu.make_async_copy(K.pdx, K.pdx_out, K.osem.at[3])
    store_pdx.start()
    prompt_sum.go(1)
    param_step(1, False)
    param_step(2, True)
    sums[3].go(2)
    K.o_pddt[...] += state_steps(K.accq, 0)[1]
    param_step(2, False)
    prompt_sum.go(2)
    for j in range(4):
        sums[j].go(3)
    store_rdbc = pltpu.make_async_copy(K.rdbc, K.rdbc_out, K.osem.at[2])
    store_rdbc.start()

    K.cb_out[0:16, :] = jnp.zeros((16, 128), F32)
    for i in range(3):
        for m in range(4):
            K.cb_out[4 * i + m : 4 * i + m + 1, :] = K.tailb[5 + i : 6 + i, 128 * m : 128 * m + 128]
    K.cb_out[16:32, :] = K.hp_sum[3, 40:56, :]
    if many:
        last = exchange(K.cb_out, K.cb_in, nt, mt, lambda k: {"tensor": lax.rem(mt + k, nt)}, 3)
        for one in last:
            one.start()
        K.cb_in[mt] = K.cb_out[...]
    for k in range(4):
        for g in range(NG):
            K.o_cw[k : k + 1, 128 * g : 128 * g + 128] = K.hp_sum[3, k * NG + g : k * NG + g + 1, :]
    K.o_hp[...] = K.hp_sum[3, 56:59, 0:NH]
    prompt_sum.go(3)
    K.o_pdbc[...] = K.pfull[...]
    if many:
        for one in last:
            one.wait()
        total = K.cb_in[0]
        for k in range(1, nt):
            total = total + K.cb_in[k]
    else:
        total = K.cb_out[...]
    for m in range(4):
        lanes = slice(128 * m, 128 * m + 128)
        for i in range(3):
            K.o_pdbc[125 + i : 126 + i, lanes] += total[4 * i + m : 4 * i + m + 1, :]
        for k in range(4):
            K.o_cbc[k : k + 1, lanes] = total[16 + 4 * k + m : 17 + 4 * k + m, :]
    stores = [store_rdx, store_out, store_rdbc, store_pdx]
    for i, name in enumerate(BIG_OUT[4:]):
        one = pltpu.make_async_copy(getattr(K, name), getattr(K, name + "_out"), K.osem.at[4 + i])
        one.start()
        stores.append(one)
    for one in stores:
        one.wait()


def finish(*refs):
    count = len(refs) // 3
    sems = refs[-1]
    come = [pltpu.make_async_copy(refs[i], refs[2 * count + i], sems.at[0, i]) for i in range(count)]
    leave = [pltpu.make_async_copy(refs[2 * count + i], refs[count + i], sems.at[1, i]) for i in range(count)]
    for one in come:
        one.start()
    for one, two in zip(come, leave):
        one.wait()
        two.start()
    for one in leave:
        one.wait()


def body(n, nt, *args):
    (px, pbc, pdt, pz, rx, rbc, rdt, rz, cw, cbc, hp, of, rlen, pcot, rcot) = args
    given = dict(px=px, pbc=pbc, pdt=pdt, pz=pz, pcot=pcot, rx=rx, rbc=rbc, rdt=rdt, rz=rz, rcot=rcot, cw=cw, cbc=cbc, hp=hp)
    sm = pl.BlockSpec(memory_space=pltpu.SMEM)
    far = pl.BlockSpec(memory_space=pl.ANY)
    shape = jax.ShapeDtypeStruct
    params = dict(vmem_limit_bytes=62 * 1024 * 1024, has_side_effects=True)
    if n > 1:
        params["collective_id"] = 0
    shapes = [shape(*SHAPES[name]) for name in BIG_OUT]
    results = pl.pallas_call(
        functools.partial(kernel, n, nt),
        out_shape=tuple(shapes),
        in_specs=[far] * len(BIG_IN) + [sm] * len(SCALARS),
        out_specs=tuple([far] * len(BIG_OUT)),
        scratch_shapes=list(scratch_table().values()),
        compiler_params=pltpu.CompilerParams(**params),
    )(*[given[name] for name in BIG_IN], of, rlen)
    results = pl.pallas_call(
        finish,
        out_shape=tuple(shapes),
        in_specs=[far] * len(shapes),
        out_specs=tuple([far] * len(shapes)),
        scratch_shapes=[pltpu.VMEM(one.shape, one.dtype) for one in shapes] + [pltpu.SemaphoreType.DMA((2, len(shapes)))],
        compiler_params=pltpu.CompilerParams(vmem_limit_bytes=62 * 1024 * 1024),
    )(*results)
    got = dict(zip(BIG_OUT, results))
    order = ("out", "pdx", "o_pdbc", "o_pddt", "rdx", "rdbc", "o_rddt", "o_cw", "o_cbc", "o_hp")
    return tuple(got[name] for name in order)


def solution(mesh):
    n = mesh.shape["dp"]
    nt = mesh.shape["tensor"]
    placed = (
        P("dp", "tensor"), P("dp", None), P("tensor", "dp"), P("dp", "tensor"),
        P("dp", "tensor"), P("dp", None), P("tensor", "dp"), P("dp", "tensor"),
        P(None, "tensor"), P(), P(None, "tensor"), P(), P("dp", None),
        P("dp", "tensor"), P("dp", "tensor"),
    )
    return jax.shard_map(
        functools.partial(body, n, nt),
        mesh=mesh,
        in_specs=placed,
        out_specs=(
            P("dp", "tensor"), P("dp", "tensor"), P("dp", None), P("tensor", "dp"),
            P("dp", "tensor"), P("dp", None), P("tensor", "dp"),
            P(None, "tensor"), P(), P(None, "tensor"),
        ),
        check_vma=False,
    )
```

```python
import functools
import types

import jax
import jax.numpy as jnp
from jax import lax
from jax.experimental import pallas as pl
from jax.experimental.pallas import tpu as pltpu
from jax.sharding import PartitionSpec as P

F32 = jnp.float32
BF = jnp.bfloat16
T = 128
NH = 20
NG = 10
NS = 256
CHD = 1280
BCW = 512
UNROLL = 10
ROW = 40
SMALL = 10


def mm(a, b, ca, cb):
    return lax.dot_general(a, b, (((ca,), (cb,)), ((), ())), preferred_element_type=F32)


def split2(a):
    hi = a.astype(BF)
    return hi, (a - hi.astype(F32)).astype(BF)


def split3(a):
    hi = a.astype(BF)
    rest = a - hi.astype(F32)
    mid = rest.astype(BF)
    return hi, mid, (rest - mid.astype(F32)).astype(BF)


def mm3(a, b, ca, cb):
    ah, al = split2(a)
    bh, bl = split2(b)
    return mm(ah, bh, ca, cb) + mm(ah, bl, ca, cb) + mm(al, bh, ca, cb)


def mmx(a, ones, ca, cb):
    hi, mid, lo = split3(a)
    return mm(hi, ones, ca, cb) + mm(mid, ones, ca, cb) + mm(lo, ones, ca, cb)


def sigmoid(v):
    return 0.5 + 0.5 * jnp.tanh(0.5 * v)


def softplus(u):
    e = jnp.exp(-jnp.abs(u))
    s = e / (2.0 + e)
    q = s * s
    poly = 1.0 + q * (1 / 3 + q * (1 / 5 + q * (1 / 7 + q * (1 / 9 + q * (1 / 11 + q / 13)))))
    return jnp.maximum(u, 0.0) + 2.0 * s * poly


def iota(shape, dim):
    return lax.broadcasted_iota(jnp.int32, shape, dim)


def fold8(a):
    return jnp.sum(a.reshape(16, 8, 128), axis=0)


BIG_IN = ("px", "pbc", "pdt", "cw", "cbc", "hp", "rdt", "pz", "pcot", "rz", "rcot", "rx", "rbc")
SCALARS = ("of", "rlen")
BIG_OUT = ("out", "pdx", "rdx", "rdbc", "o_pdbc", "o_pddt", "o_rddt", "o_cw", "o_cbc", "o_hp")
SHAPES = dict(
    px=((T, CHD), BF), pbc=((T, BCW), BF), pz=((T, CHD), BF), pcot=((T, CHD), BF),
    rx=((512, CHD), BF), rbc=((512, BCW), BF), rz=((512, CHD), BF), rcot=((512, CHD), BF),
    pdt=((NH, T), F32), rdt=((NH, 512), F32), cw=((4, CHD), F32), cbc=((4, BCW), F32), hp=((3, NH), F32),
    o_pdbc=((T, BCW), F32), o_pddt=((NH, T), F32), o_rddt=((NH, 512), F32), o_cw=((4, CHD), F32),
    o_cbc=((4, BCW), F32), o_hp=((3, NH), F32),
    out=((512, CHD), BF), pdx=((T, CHD), BF), rdx=((512, CHD), BF), rdbc=((512, BCW), F32),
)


def scratch_table():
    v = pltpu.VMEM
    dma = pltpu.SemaphoreType.DMA
    table = {name: v(*SHAPES[name]) for name in BIG_IN + BIG_OUT}
    for one in "tfbv":
        rows = {"t": SMALL, "f": ROW, "b": ROW, "v": SMALL}[one]
        for part in "shlr":
            table[one + part] = v((32, rows, 128), F32)
    table.update(
        hp_sum=v((4, 64, 128), F32), par_in=v((3, 4, 64, 128), F32), cb_in=v((4, 32, 128), F32), cb_out=v((32, 128), F32),
        rsum=v((512, BCW), F32), rrecv=v((4, 2, 64, BCW), F32),
        psum=v((T, BCW), F32), pfull=v((T, BCW), F32), precv=v((2, 64, BCW), F32),
        invv=v((1, 128), jnp.int32), inv=pltpu.SMEM((1, 128), jnp.int32),
        adt=v((NH, T), F32),
        dtr=v((6, NH, T), F32), sig=v((6, NH, T), F32), lr=v((6, NH, T), F32), cumr=v((6, NH, T), F32),
        tmp=v((6, 128, 128), F32), col=v((2, NH, 1), F32), dex=v((1, CHD), F32),
        cumB=v((6 * NH, T, T), F32), dtE=v((6 * T, CHD), F32),
        R=v((NG, 512, 128), BF), Gcol=v((12, T, T), F32), dGcol=v((12, T, T), F32),
        B=v((6, T, NS), F32), C=v((5, T, NS), F32), Cb=v((5, T, NS), BF), gpb=v((6 * T, BCW), F32),
        G=v((5, T, T), F32), dG=v((5, T, T), F32), acc=v((6, T, 128), F32), accq=v((T, 128), F32),
        xs=v((10, 136, 128), F32), ds=v((10, 144, 128), F32),
        tailx=v((8, CHD), F32), tailb=v((8, BCW), F32), dtailx=v((8, CHD), F32), dtailb=v((8, BCW), F32),
        dw=v((4, 8, CHD), F32), dwb=v((4, 8, BCW), F32), dD=v((8, CHD), F32),
        pxc=v((T, CHD), F32), pgp=v((T, CHD), F32), pdxf=v((T, CHD), F32),
        live=v((512, 128), F32), dy=v((512, CHD), F32), sz=v((512, CHD), F32),
        edy=v((512, CHD), BF), ee=v((512, CHD), F32),
        S=v((CHD, NS), BF), dS=v((CHD, NS), BF),
        dlr=v((NH, T), F32), ddr=v((NH, T), F32),
        sem=dma((8, 2, 32)), tsem=dma((16, 2)), gsem=dma((4, 2, 4)), isem=dma((len(BIG_IN) + 1,)), osem=dma((len(BIG_OUT),)),
    )
    return table


def kernel(n, nt, *refs):
    names = [name + "_in" for name in BIG_IN] + list(SCALARS)
    names += [name + "_out" for name in BIG_OUT] + list(scratch_table())
    K = types.SimpleNamespace(**dict(zip(names, refs)))
    me = lax.axis_index("dp")
    mt = lax.axis_index("tensor")
    left = iota((T, 128), 1) < 64
    lower = iota((T, T), 0) >= iota((T, T), 1)
    mesh_ids = pl.DeviceIdType.MESH
    many = n > 1

    if many:
        barrier = pltpu.get_barrier_semaphore()

        def greet(k):
            pl.semaphore_signal(barrier, inc=1, device_id={"dp": lax.rem(me + k, n)}, device_id_type=mesh_ids)

        pl.loop(1, n)(greet)
        for k in range(1, nt):
            pl.semaphore_signal(barrier, inc=1, device_id={"tensor": lax.rem(mt + k, nt)}, device_id_type=mesh_ids)

    loads = {
        name: pltpu.make_async_copy(getattr(K, name + "_in"), getattr(K, name), K.isem.at[i])
        for i, name in enumerate(BIG_IN)
    }
    for name in BIG_IN:
        loads[name].start()

    class Relay:
        def __init__(self, key, sem, table):
            self.s, self.h, self.l, self.r = (getattr(K, key + part) for part in "shlr")
            self.sem = sem
            self.table = table

        def copy(self, src, dst, sem):
            def one(k):
                peer = lax.rem(me + k, n)
                return pltpu.make_async_remote_copy(
                    src_ref=src.at[peer], dst_ref=dst.at[me], send_sem=K.sem.at[sem, 0, k], recv_sem=K.sem.at[sem, 1, k],
                    device_id={"dp": peer}, device_id_type=mesh_ids,
                )

            return one

        def send(self):
            if many:
                one = self.copy(self.s, self.h, self.sem)
                pl.loop(1, n)(lambda k: one(k).start())
                self.h[me] = self.s[me]

        def turn(self):
            if many:
                one = self.copy(self.s, self.h, self.sem)
                pl.loop(1, n)(lambda k: one(k).wait())

                def pick(d):
                    self.l[d] = self.h[self.table(d)]

                pl.loop(0, n)(pick)
                two = self.copy(self.l, self.r, self.sem + 1)
                pl.loop(1, n)(lambda k: two(k).start())
                self.r[me] = self.l[me]

        def end(self):
            if many:
                two = self.copy(self.l, self.r, self.sem + 1)
                pl.loop(1, n)(lambda k: two(k).wait())
            else:
                self.r[...] = self.s[...]

    forth = lambda d: K.of[d]
    home = lambda d: K.inv[0, d]
    rt, rf = Relay("t", 0, forth), Relay("f", 2, forth)
    rb, rd = Relay("b", 4, home), Relay("v", 6, home)

    def lanes_of(g):
        return pl.ds(pl.multiple_of(g * 128, 128), 128)

    def rows_of(q):
        return pl.ds(pl.multiple_of(q * T, T), T)

    def scatter_rows(ref, k, half, tile):
        spot = pl.ds(pl.multiple_of(8 * k, 8), 8)
        for i in range(16):
            ref[2 * i + half, spot, :] = tile[8 * i : 8 * i + 8, :]

    def gather_rows(ref, k, half):
        spot = pl.ds(pl.multiple_of(8 * k, 8), 8)
        return jnp.concatenate([ref[2 * i + half, spot, :] for i in range(16)], axis=0)

    def tail_rows(rows_x, rows_b):
        for r in range(42):
            i, m = divmod(r, 14)
            ref, m = (rows_x, m) if m < 10 else (rows_b, m - 10)
            yield r, ref, slice(5 + i, 6 + i), slice(128 * m, 128 * m + 128)

    for name in BIG_IN[:7]:
        loads[name].wait()
    K.tailx[...] = K.px[112:128, :].astype(F32)[8:16, :]
    K.tailb[...] = K.pbc[112:128, :].astype(F32)[8:16, :]
    K.ts[:, 8:10, :] = jnp.zeros((32, 2, 128), F32)
    for r, ref, row, lanes in tail_rows(K.tailx, K.tailb):
        K.ts[r // 2, 8 + r % 2 : 9 + r % 2, :] = ref[row, lanes]
    for h in range(NH):
        r = 42 + h
        K.ts[r // 2, 8 + r % 2 : 9 + r % 2, :] = K.pdt[h : h + 1, :]
    for half in range(2):
        scatter_rows(K.ts, 0, half, K.pbc[:, 128 * half : 128 * half + 128].astype(F32))

    def pack_x(k):
        for half in range(2):
            scatter_rows(K.fs, k, half, K.px[:, lanes_of(5 * half + k)].astype(F32))

    if many:
        pl.semaphore_wait(barrier, n - 1 + nt - 1)
    rt.send()
    pl.loop(0, 5)(pack_x)
    rf.send()

    tri = (iota((T, T), 0) <= iota((T, T), 1)).astype(F32).astype(BF)
    trir = (iota((T, T), 0) >= iota((T, T), 1)).astype(F32).astype(BF)
    tris = (iota((T, T), 0) < iota((T, T), 1)).astype(F32).astype(BF)
    eye = iota((NH, NH), 0) == iota((NH, NH), 1)

    lane = iota((1, 128), 1)
    back_to = jnp.zeros((1, 128), jnp.int32)
    for d in range(n):
        back_to = jnp.where(lane == K.of[d], d, back_to)
    K.invv[...] = back_to
    inv_copy = pltpu.make_async_copy(K.invv, K.inv, K.isem.at[len(BIG_IN)])
    inv_copy.start()

    def column(row):
        return jnp.sum(jnp.where(eye, jnp.broadcast_to(K.hp[row : row + 1, :], (NH, NH)), 0.0), axis=1, keepdims=True)

    K.col[0] = -jnp.exp(column(0))
    K.col[1] = column(1)
    for g in range(NG):
        K.dex[:, 128 * g : 128 * g + 128] = jnp.where(
            lane < 64, K.hp[2:3, 2 * g : 2 * g + 1], K.hp[2:3, 2 * g + 1 : 2 * g + 2]
        )
    for j in range(4):
        K.live[j * T : j * T + T, :] = jnp.where(iota((T, 128), 0) < K.rlen[0, j], 1.0, 0.0)

    def make_R(g):
        r = iota((512, 128), 0)
        want = 2 * g + jnp.where((r & 127) >= 64, 1, 0) + jnp.where(r >= 256, 32, 0)
        K.R[g] = (iota((512, 128), 1) == want).astype(F32).astype(BF)

    pl.loop(0, NG)(make_R)
    for name in ("dG", "acc", "accq", "dw", "dwb", "dD", "dtailx", "dtailb", "dGcol", "dlr", "ddr", "ds", "tmp"):
        ref = getattr(K, name)
        ref[...] = jnp.zeros(ref.shape, F32)

    def step_tables(dt_ref, ats, qs):
        every = list(zip(ats, qs))
        for at, q in every:
            u = dt_ref[:, at * T : at * T + T] + K.col[1]
            dt = softplus(u)
            lr = K.col[0] * dt
            cum = mmx(lr, tri, 1, 0)
            K.sig[q] = 1.0 / (1.0 + jnp.exp(-u))
            K.lr[q] = lr
            K.cumr[q] = cum
            K.tmp[q, 0:NH, :] = cum
            K.tmp[q, 32 : 32 + NH, :] = dt
        for at, q in every:
            cols = K.tmp[q].T
            for h in range(NH):
                K.cumB[q * NH + h] = jnp.broadcast_to(cols[:, h : h + 1], (T, T))
            for g in range(NG):
                a = 32 + 2 * g
                K.dtE[q * T : q * T + T, 128 * g : 128 * g + 128] = jnp.where(
                    left, jnp.broadcast_to(cols[:, a : a + 1], (T, 128)), jnp.broadcast_to(cols[:, a + 1 : a + 2], (T, 128))
                )

    def conv(x, tail, w, u=0):
        K.xs[u, 0:8, :] = tail
        K.xs[u, 8:136, :] = x
        v = w[0] * K.xs[u, 5:133, :] + w[1] * K.xs[u, 6:134, :] + w[2] * K.xs[u, 7:135, :] + w[3] * x
        s = sigmoid(v)
        xc = v * s
        return xc, s + xc * (1.0 - s)

    def conv_taps(dv, dw_ref, lanes, u=0):
        for k in range(4):
            dw_ref[k, :, lanes] += fold8(dv * K.xs[u, 5 + k : 133 + k, :])

    def tail_back(dv, w, tail_ref, lanes, u):
        K.ds[u, 8:16, :] = dv
        tail_ref[:, lanes] += w[0] * K.ds[u, 3:11, :] + w[1] * K.ds[u, 2:10, :] + w[2] * K.ds[u, 1:9, :]

    def conv_back(dv, w, u=0):
        K.ds[u, 8:136, :] = dv
        return w[3] * dv + w[2] * K.ds[u, 9:137, :] + w[1] * K.ds[u, 10:138, :] + w[0] * K.ds[u, 11:139, :]

    def taps(ref, lanes):
        return [ref[k : k + 1, lanes] for k in range(4)]

    no_tail = jnp.zeros((8, 128), F32)

    def bc_forward(bc_ref, at, q, tail, u=0):
        for m in range(4):
            lanes = slice(128 * m, 128 * m + 128)
            xc, gp = conv(bc_ref[rows_of(at), lanes].astype(F32), tail(lanes), taps(K.cbc, lanes), m)
            K.gpb[rows_of(q), lanes] = gp
            if m < 2:
                K.B[q, :, lanes] = xc
            else:
                half = slice(128 * (m - 2), 128 * (m - 2) + 128)
                K.C[q, :, half] = xc
                K.Cb[q, :, half] = xc.astype(BF)
        K.G[q] = jnp.where(lower, mm3(K.C[q], K.B[q], 1, 1), 0.0)

    def bc_back(bc_ref, at, q, tail, dc_more, o_ref):
        dgm = jnp.where(lower, K.dG[q], 0.0)
        dc = mm3(dgm, K.B[q], 1, 0) + dc_more
        db = mm3(dgm, K.C[q], 0, 0)
        for m in range(4):
            lanes = slice(128 * m, 128 * m + 128)
            d = db[:, lanes] if m < 2 else dc[:, 128 * (m - 2) : 128 * (m - 2) + 128]
            dv = d * K.gpb[rows_of(q), lanes]
            K.xs[m, 0:8, :] = tail(lanes)
            K.xs[m, 8:136, :] = bc_ref[rows_of(at), lanes].astype(F32)
            conv_taps(dv, K.dwb, lanes, m)
            o_ref[rows_of(at), lanes] = conv_back(dv, taps(K.cbc, lanes), m)

    def cum_pair(q, g):
        return jnp.where(left, K.cumB[q * NH + 2 * g], K.cumB[q * NH + 2 * g + 1])

    def attend(q, g, xc, dy, dt):
        xd = dt * xc
        x2 = jnp.concatenate([jnp.where(left, xd, 0.0).astype(BF), jnp.where(left, 0.0, xd).astype(BF)], axis=0)
        d2 = jnp.concatenate([jnp.where(left, dy, 0.0).astype(BF), jnp.where(left, 0.0, dy).astype(BF)], axis=0)
        xdb = xd.astype(BF)
        dyb = dy.astype(BF)
        scores = K.G[q]
        decay = [
            jnp.exp(jnp.minimum(K.cumB[q * NH + 2 * g + i] - K.cumr[q, pl.ds(2 * g + i, 1), :], 0.0)) for i in range(2)
        ]
        mix = [(scores * one).astype(BF) for one in decay]
        yin = mm(jnp.concatenate(mix, axis=1), x2, 1, 0)
        dxd = mm(jnp.concatenate(mix, axis=0), d2, 0, 0)
        dmix = mm(dyb, x2, 1, 1)
        K.dG[q] += dmix[:, :T] * decay[0] + dmix[:, T:] * decay[1]
        return yin, dxd, xdb.astype(F32), dyb.astype(F32)

    def reduce_heads(g, first, second=None):
        parts = list(split2(first))
        if second is not None:
            parts += split2(second)
        return mm(jnp.concatenate(parts, axis=1), K.R[g, : 128 * len(parts), :], 1, 0)

    def steps_back(q, o_ref, at):
        a = K.acc[q].T
        dlr = mmx(a[0:NH, :], trir, 1, 0)
        draw = (a[32 : 32 + NH, :] + K.col[0] * dlr) * K.sig[q]
        o_ref[:, pl.ds(pl.multiple_of(at * T, T), T)] = draw
        K.dlr[...] += K.lr[q] * dlr
        K.ddr[...] += draw

    def state_steps(acc, q):
        a = acc[...].T
        dlr = mmx(a[0:NH, :], tris, 1, 0)
        return dlr, (a[32 : 32 + NH, :] + K.col[0] * dlr) * K.sig[q]

    step_tables(K.pdt, [0], [0])
    bc_forward(K.pbc, 0, 0, lambda lanes: no_tail)
    loads["pz"].wait()
    loads["pcot"].wait()

    def prompt_local(i):
        for u in range(UNROLL):
            g = i * UNROLL + u
            lanes = lanes_of(g)
            w = taps(K.cw, lanes)
            xc, gp = conv(K.px[:, lanes].astype(F32), no_tail, w, u)
            K.pxc[:, lanes] = xc
            K.pgp[:, lanes] = gp
            z = K.pz[:, lanes].astype(F32)
            dy = K.pcot[:, lanes].astype(F32) * (z * sigmoid(z))
            dt = K.dtE[0:T, lanes]
            yin, dxd, xdr, dyr = attend(0, g, xc, dy, dt)
            K.acc[0] += reduce_heads(g, dyr * yin - xdr * dxd, xc * dxd)
            K.dD[:, lanes] += fold8(dy * xc)
            dv = (dt * dxd + K.dex[:, lanes] * dy) * gp
            conv_taps(dv, K.dw, lanes, u)
            K.pdxf[:, lanes] = conv_back(dv, w, u)

    pl.loop(0, NG // UNROLL)(prompt_local)
    bc_back(K.pbc, 0, 0, lambda lanes: no_tail, 0.0, K.psum)
    steps_back(0, K.o_pddt, 0)

    rt.turn()

    step_tables(K.rdt, [0, 1, 2, 3], [1, 2, 3, 4])
    loads["rz"].wait()
    loads["rcot"].wait()

    def gates(i):
        j = i // NG
        g = lax.rem(i, NG)
        lanes = lanes_of(g)
        rows = rows_of(j)
        z = K.rz[rows, lanes].astype(F32)
        sz = z * sigmoid(z)
        dy = K.rcot[rows, lanes].astype(F32) * (sz * K.live[rows, :])
        e = jnp.exp(cum_pair(j + 1, g))
        K.sz[rows, lanes] = sz
        K.dy[rows, lanes] = dy
        K.ee[rows, lanes] = e
        K.edy[rows, lanes] = (e * dy).astype(BF)

    pl.loop(0, 4 * NG, unroll=2)(gates)
    rf.turn()
    loads["rx"].wait()
    loads["rbc"].wait()
    inv_copy.wait()
    rt.end()

    for r, ref, row, lanes in tail_rows(K.tailx, K.tailb):
        ref[row, lanes] = K.tr[r // 2, 8 + r % 2 : 9 + r % 2, :]
    for h in range(NH):
        r = 42 + h
        K.adt[h : h + 1, :] = K.tr[r // 2, 8 + r % 2 : 9 + r % 2, :]
    for j in range(4):
        bc_forward(K.rbc, j, j + 1, lambda lanes: K.tailb[:, lanes])
    for half in range(2):
        lanes = slice(128 * half, 128 * half + 128)
        xc, gp = conv(gather_rows(K.tr, 0, half), no_tail, taps(K.cbc, lanes), half)
        K.B[5, :, lanes] = xc
        K.gpb[5 * T : 6 * T, lanes] = gp

    def state_grad(k):
        bh = K.B[5].astype(BF)
        for half in range(2):
            lanes = lanes_of(5 * half + k)
            ds = mm(K.edy[:, lanes], K.Cb[1:5].reshape(4 * T, NS), 0, 0).astype(BF)
            K.dS[lanes, :] = ds
            scatter_rows(K.bs, k, half, mm(bh, ds, 1, 1))

    pl.loop(0, 5)(state_grad)
    rb.send()
    step_tables(K.adt, [0], [5])

    row8 = iota((8, 128), 0)
    for j in range(4):
        for t in range(3):
            K.Gcol[3 * j + t] = jnp.broadcast_to(K.G[j + 1, :, t : t + 1], (T, T))

    def first_rows(j):
        def five(i):
            for u in range(UNROLL):
                g = i * UNROLL + u
                lanes = lanes_of(g)
                w = taps(K.cw, lanes)
                K.xs[u, 0:8, :] = K.tailx[:, lanes]
                K.xs[u, 8:24, :] = K.rx[pl.ds(j * T, 16), lanes].astype(F32)
                v = (w[0] * K.xs[u, 5:13, :] + w[1] * K.xs[u, 6:14, :] + w[2] * K.xs[u, 7:15, :]
                     + w[3] * K.xs[u, 8:16, :])
                sg = sigmoid(v)
                xc = v * sg
                gp = sg + xc * (1.0 - sg)
                dt = K.dtE[pl.ds((j + 1) * T, 8), lanes]
                xd = dt * xc
                dy = K.dy[rows_of(j), lanes]
                cum = cum_pair(j + 1, g)
                dxd = jnp.zeros((8, 128), F32)
                for t in range(3):
                    m = jnp.exp(jnp.minimum(cum - cum[t : t + 1, :], 0.0)) * dy
                    K.dGcol[3 * j + t] += m * xd[t : t + 1, :]
                    dxd = jnp.where(row8 == t, jnp.sum(K.Gcol[3 * j + t] * m, axis=0, keepdims=True), dxd)
                dv = (dt * dxd + K.dex[:, lanes] * dy[0:8, :]) * gp
                tail_back(jnp.where(row8 < 3, dv, 0.0), w, K.dtailx, lanes, u)

        pl.loop(0, NG // UNROLL)(five)

    def first_bc_rows(j):
        more = mm(K.edy[pl.ds(j * T, 16), :], K.S[...], 1, 0)[0:8, :]
        r8 = iota((8, NS), 0)
        dc = more
        db = jnp.zeros((8, NS), F32)
        for t in range(3):
            col = jnp.sum(K.dGcol[3 * j + t], axis=1, keepdims=True)
            col = jnp.where(iota((T, 1), 0) >= t, col, 0.0)
            dc = dc + col[0:8, :] * K.B[j + 1, t : t + 1, :]
            db = jnp.where(r8 == t, jnp.sum(col * K.C[j + 1], axis=0, keepdims=True), db)
        for m in range(4):
            lanes = slice(128 * m, 128 * m + 128)
            d = db[:, lanes] if m < 2 else dc[:, 128 * (m - 2) : 128 * (m - 2) + 128]
            dv = jnp.where(row8 < 3, d * K.gpb[pl.ds((j + 1) * T, 8), lanes], 0.0)
            tail_back(dv, taps(K.cbc, lanes), K.dtailb, lanes, m)

    for j in range(4):
        first_rows(j)

    def resp_local(j):
        def five(i):
            for u in range(UNROLL):
                g = i * UNROLL + u
                lanes = lanes_of(g)
                rows = rows_of(j)
                w = taps(K.cw, lanes)
                xc, gp = conv(K.rx[rows, lanes].astype(F32), K.tailx[:, lanes], w, u)
                dy = K.dy[rows, lanes]
                dt = K.dtE[rows_of(j + 1), lanes]
                yin, dxd, xdr, dyr = attend(j + 1, g, xc, dy, dt)
                gain = K.dex[:, lanes]
                y = yin + gain * xc
                steps = dyr * yin - xdr * dxd
                cs = mm(K.Cb[j + 1], K.S[lanes, :], 1, 1)
                K.out[rows, lanes] = ((y + K.ee[rows, lanes] * cs) * K.sz[rows, lanes]).astype(BF)
                steps = steps + K.edy[rows, lanes].astype(F32) * cs
                K.acc[j + 1] += reduce_heads(g, steps, xc * dxd)
                K.dD[:, lanes] += fold8(dy * xc)
                dv = (dt * dxd + gain * dy) * gp
                conv_taps(dv, K.dw, lanes, u)
                K.rdx[rows, lanes] = conv_back(dv, w, u).astype(BF)

        pl.loop(0, NG // UNROLL)(five)

    def resp_bc_back(j):
        more = mm(K.edy[rows_of(j), :], K.S[...], 1, 0)
        bc_back(K.rbc, j, j + 1, lambda lanes: K.tailb[:, lanes], more, K.rsum)

    core = lax.rem(mt, 2)
    mate = mt + 1 - 2 * core
    across = lax.rem(mt + 2, 4)

    class TensorSum:
        def __init__(self, buf, full, recv, base, at):
            mine = pl.ds(pl.multiple_of(base + core * 64, 8), 64)
            other = pl.ds(pl.multiple_of(base + (1 - core) * 64, 8), 64)
            self.buf, self.full, self.recv, self.base, self.mine = buf, full, recv, base, mine
            plan = ((buf.at[other, :], recv.at[0], mate), (buf.at[mine, :], recv.at[1], across),
                    (buf.at[mine, :], full.at[mine, :], mate))
            self.steps = [
                pltpu.make_async_remote_copy(
                    src_ref=src, dst_ref=dst, send_sem=K.tsem.at[at + i, 0], recv_sem=K.tsem.at[at + i, 1],
                    device_id={"tensor": peer}, device_id_type=mesh_ids,
                )
                for i, (src, dst, peer) in enumerate(plan)
            ] if many else None

        def go(self, stage):
            if not many:
                if stage == 0:
                    rows = pl.ds(self.base, T)
                    self.full[rows, :] = self.buf[rows, :]
                return
            if stage > 0:
                self.steps[stage - 1].wait()
            if stage in (1, 2):
                self.buf[self.mine, :] += self.recv[stage - 1]
            if stage == 2:
                self.full[self.mine, :] = self.buf[self.mine, :]
            if stage < 3:
                self.steps[stage].start()

    sums = [TensorSum(K.rsum, K.rdbc, K.rrecv.at[j], j * T, 3 * j) for j in range(4)]

    rf.end()

    def adopt(k, dbp):
        bh, bl = split2(K.B[5])
        for half in range(2):
            g = 5 * half + k
            lanes = lanes_of(g)
            xc, gp = conv(gather_rows(K.fr, k, half), no_tail, taps(K.cw, lanes), half)
            cum = cum_pair(5, g)
            lv = jnp.exp(cum[T - 1 : T, :] - cum)
            dt = K.dtE[5 * T : 6 * T, lanes]
            xd = dt * xc
            xh, xl = split2(lv * xd)
            K.S[lanes, :] = (mm(xh, bh, 0, 0) + mm(xh, bl, 0, 0) + mm(xl, bh, 0, 0)).astype(BF)
            dbp = dbp + mm(xh, K.dS[lanes, :], 1, 0)
            lu = lv * gather_rows(K.bs, k, half)
            K.acc[5] += reduce_heads(g, xd * lu, xc * lu)
            conv_taps(dt * lu * gp, K.dw, lanes, half)
        return dbp

    dbp = lax.fori_loop(0, 5, adopt, jnp.zeros((T, NS), F32))
    for half in range(2):
        lanes = slice(128 * half, 128 * half + 128)
        scatter_rows(K.vs, 0, half, dbp[:, lanes])
        K.xs[half, 0:8, :] = no_tail
        K.xs[half, 8:136, :] = gather_rows(K.tr, 0, half)
        conv_taps(dbp[:, lanes] * K.gpb[5 * T : 6 * T, lanes], K.dwb, lanes, half)
    for j in range(4):
        first_bc_rows(j)
    K.vs[:, 8:10, :] = jnp.zeros((32, 2, 128), F32)
    for r, ref, row, lanes in tail_rows(K.dtailx, K.dtailb):
        K.vs[r // 2, 8 + r % 2 : 9 + r % 2, :] = ref[row, lanes]
    rd.send()
    dlr, draw = state_steps(K.acc.at[5], 5)
    K.dlr[...] += K.lr[5] * dlr
    K.ddr[...] += draw

    resp_local(0)
    resp_bc_back(0)
    sums[0].go(0)
    rb.turn()
    resp_local(1)
    resp_bc_back(1)
    sums[0].go(1)
    sums[1].go(0)
    rd.turn()
    resp_local(2)
    resp_bc_back(2)
    sums[0].go(2)
    sums[1].go(1)
    sums[2].go(0)
    resp_local(3)
    resp_bc_back(3)
    sums[3].go(0)
    sums[1].go(2)
    sums[2].go(1)
    store_rdx = pltpu.make_async_copy(K.rdx, K.rdx_out, K.osem.at[0])
    store_rdx.start()
    store_out = pltpu.make_async_copy(K.out, K.out_out, K.osem.at[1])
    store_out.start()

    for j in range(4):
        steps_back(j + 1, K.o_rddt, j)
    K.hp_sum[0] = jnp.zeros((64, 128), F32)
    for k in range(4):
        total = jnp.sum(K.dw[k], axis=0, keepdims=True)
        for g in range(NG):
            K.hp_sum[0, k * NG + g : k * NG + g + 1, :] = total[:, 128 * g : 128 * g + 128]
        total = jnp.sum(K.dwb[k], axis=0, keepdims=True)
        for m in range(4):
            K.hp_sum[0, 40 + 4 * k + m : 41 + 4 * k + m, :] = total[:, 128 * m : 128 * m + 128]
    skip = jnp.zeros((8, 128), F32)
    for g in range(NG):
        skip = skip + mm(jnp.concatenate(split2(K.dD[:, 128 * g : 128 * g + 128]), axis=1), K.R[g, :256, :], 1, 0)
    spread_eye = iota((NH, 128), 0) == iota((NH, 128), 1)

    def as_row(ref):
        total = jnp.sum(ref[...], axis=1, keepdims=True)
        return jnp.sum(jnp.where(spread_eye, jnp.broadcast_to(total, (NH, 128)), 0.0), axis=0, keepdims=True)

    K.hp_sum[0, 56:57, :] = as_row(K.dlr)
    K.hp_sum[0, 57:58, :] = as_row(K.ddr)
    K.hp_sum[0, 58:59, :] = jnp.sum(skip, axis=0, keepdims=True)

    z_at, x_at, y_at = lax.rem(me, 4), lax.rem(me // 4, 2), me // 8
    axes = (
        (4, z_at, lambda k: {"dp": me - z_at + lax.rem(z_at + k, 4)}),
        (4, y_at, lambda k: {"dp": me - 8 * y_at + 8 * lax.rem(y_at + k, 4)}),
        (2, x_at, lambda k: {"dp": me + 4 - 8 * x_at}),
    )

    def exchange(src, hold, size, at, peer, sem):
        return [
            pltpu.make_async_remote_copy(
                src_ref=src, dst_ref=hold.at[at], send_sem=K.gsem.at[sem, 0, k], recv_sem=K.gsem.at[sem, 1, k],
                device_id=peer(k), device_id_type=mesh_ids,
            )
            for k in range(1, size)
        ]

    def param_step(i, start):
        size, at, peer = axes[i]
        if not many:
            if not start:
                K.hp_sum[i + 1] = K.hp_sum[i]
            return
        copies = exchange(K.hp_sum.at[i], K.par_in.at[i], size, at, peer, i)
        if start:
            for one in copies:
                one.start()
            K.par_in[i, at] = K.hp_sum[i]
        else:
            for one in copies:
                one.wait()
            total = K.par_in[i, 0]
            for k in range(1, size):
                total = total + K.par_in[i, k]
            K.hp_sum[i + 1] = total

    param_step(0, True)
    rd.end()
    for half in range(2):
        lanes = slice(128 * half, 128 * half + 128)
        dv = gather_rows(K.vr, 0, half) * K.gpb[0:T, lanes]
        K.psum[:, lanes] += conv_back(dv, taps(K.cbc, lanes), u=half)
    prompt_sum = TensorSum(K.psum, K.pfull, K.precv, 0, 12)
    prompt_sum.go(0)
    sums[3].go(1)
    sums[2].go(2)
    param_step(0, False)
    param_step(1, True)

    def prompt_final(k):
        for half in range(2):
            g = 5 * half + k
            lanes = lanes_of(g)
            cum = cum_pair(0, g)
            lu = jnp.exp(cum[T - 1 : T, :] - cum) * gather_rows(K.br, k, half)
            dt = K.dtE[0:T, lanes]
            xlu = K.pxc[:, lanes] * lu
            K.accq[...] += reduce_heads(g, dt * xlu, xlu)
            K.pdxf[:, lanes] += conv_back(dt * lu * K.pgp[:, lanes], taps(K.cw, lanes), u=half)

    rb.end()
    pl.loop(0, 5)(prompt_final)
    K.tailx[...] = jnp.zeros((8, CHD), F32)
    K.tailb[...] = jnp.zeros((8, BCW), F32)
    for r, ref, row, lanes in tail_rows(K.tailx, K.tailb):
        ref[row, lanes] = K.vr[r // 2, 8 + r % 2 : 9 + r % 2, :]
    K.pdxf[120:128, :] += K.tailx[...]
    K.pdx[...] = K.pdxf[...].astype(BF)
    store_pdx = pltpu.make_async_copy(K.pdx, K.pdx_out, K.osem.at[3])
    store_pdx.start()
    prompt_sum.go(1)
    param_step(1, False)
    param_step(2, True)
    sums[3].go(2)
    K.o_pddt[...] += state_steps(K.accq, 0)[1]
    param_step(2, False)
    prompt_sum.go(2)
    for j in range(4):
        sums[j].go(3)
    store_rdbc = pltpu.make_async_copy(K.rdbc, K.rdbc_out, K.osem.at[2])
    store_rdbc.start()

    K.cb_out[0:16, :] = jnp.zeros((16, 128), F32)
    for i in range(3):
        for m in range(4):
            K.cb_out[4 * i + m : 4 * i + m + 1, :] = K.tailb[5 + i : 6 + i, 128 * m : 128 * m + 128]
    K.cb_out[16:32, :] = K.hp_sum[3, 40:56, :]
    if many:
        last = exchange(K.cb_out, K.cb_in, nt, mt, lambda k: {"tensor": lax.rem(mt + k, nt)}, 3)
        for one in last:
            one.start()
        K.cb_in[mt] = K.cb_out[...]
    for k in range(4):
        for g in range(NG):
            K.o_cw[k : k + 1, 128 * g : 128 * g + 128] = K.hp_sum[3, k * NG + g : k * NG + g + 1, :]
    K.o_hp[...] = K.hp_sum[3, 56:59, 0:NH]
    prompt_sum.go(3)
    K.o_pdbc[...] = K.pfull[...]
    if many:
        for one in last:
            one.wait()
        total = K.cb_in[0]
        for k in range(1, nt):
            total = total + K.cb_in[k]
    else:
        total = K.cb_out[...]
    for m in range(4):
        lanes = slice(128 * m, 128 * m + 128)
        for i in range(3):
            K.o_pdbc[125 + i : 126 + i, lanes] += total[4 * i + m : 4 * i + m + 1, :]
        for k in range(4):
            K.o_cbc[k : k + 1, lanes] = total[16 + 4 * k + m : 17 + 4 * k + m, :]
    stores = [store_rdx, store_out, store_rdbc, store_pdx]
    for i, name in enumerate(BIG_OUT[4:]):
        one = pltpu.make_async_copy(getattr(K, name), getattr(K, name + "_out"), K.osem.at[4 + i])
        one.start()
        stores.append(one)
    for one in stores:
        one.wait()


def finish(*refs):
    count = len(refs) // 3
    sems = refs[-1]
    come = [pltpu.make_async_copy(refs[i], refs[2 * count + i], sems.at[0, i]) for i in range(count)]
    leave = [pltpu.make_async_copy(refs[2 * count + i], refs[count + i], sems.at[1, i]) for i in range(count)]
    for one in come:
        one.start()
    for one, two in zip(come, leave):
        one.wait()
        two.start()
    for one in leave:
        one.wait()


def body(n, nt, *args):
    (px, pbc, pdt, pz, rx, rbc, rdt, rz, cw, cbc, hp, of, rlen, pcot, rcot) = args
    given = dict(px=px, pbc=pbc, pdt=pdt, pz=pz, pcot=pcot, rx=rx, rbc=rbc, rdt=rdt, rz=rz, rcot=rcot, cw=cw, cbc=cbc, hp=hp)
    sm = pl.BlockSpec(memory_space=pltpu.SMEM)
    far = pl.BlockSpec(memory_space=pl.ANY)
    shape = jax.ShapeDtypeStruct
    params = dict(vmem_limit_bytes=62 * 1024 * 1024, has_side_effects=True)
    if n > 1:
        params["collective_id"] = 0
    shapes = [shape(*SHAPES[name]) for name in BIG_OUT]
    results = pl.pallas_call(
        functools.partial(kernel, n, nt),
        out_shape=tuple(shapes),
        in_specs=[far] * len(BIG_IN) + [sm] * len(SCALARS),
        out_specs=tuple([far] * len(BIG_OUT)),
        scratch_shapes=list(scratch_table().values()),
        compiler_params=pltpu.CompilerParams(**params),
    )(*[given[name] for name in BIG_IN], of, rlen)
    results = pl.pallas_call(
        finish,
        out_shape=tuple(shapes),
        in_specs=[far] * len(shapes),
        out_specs=tuple([far] * len(shapes)),
        scratch_shapes=[pltpu.VMEM(one.shape, one.dtype) for one in shapes] + [pltpu.SemaphoreType.DMA((2, len(shapes)))],
        compiler_params=pltpu.CompilerParams(vmem_limit_bytes=62 * 1024 * 1024),
    )(*results)
    got = dict(zip(BIG_OUT, results))
    order = ("out", "pdx", "o_pdbc", "o_pddt", "rdx", "rdbc", "o_rddt", "o_cw", "o_cbc", "o_hp")
    return tuple(got[name] for name in order)


def solution(mesh):
    n = mesh.shape["dp"]
    nt = mesh.shape["tensor"]
    placed = (
        P("dp", "tensor"), P("dp", None), P("tensor", "dp"), P("dp", "tensor"),
        P("dp", "tensor"), P("dp", None), P("tensor", "dp"), P("dp", "tensor"),
        P(None, "tensor"), P(), P(None, "tensor"), P(), P("dp", None),
        P("dp", "tensor"), P("dp", "tensor"),
    )
    return jax.shard_map(
        functools.partial(body, n, nt),
        mesh=mesh,
        in_specs=placed,
        out_specs=(
            P("dp", "tensor"), P("dp", "tensor"), P("dp", None), P("tensor", "dp"),
            P("dp", "tensor"), P("dp", None), P("tensor", "dp"),
            P(None, "tensor"), P(), P(None, "tensor"),
        ),
        check_vma=False,
    )
```
